32 devices in a mesh: visit: 8 (over y, x, core), sky: 4 (over z).
Axes of the slice: x: 2, y: 2, z: 4, core: 2. Of those that a mesh axis runs over, the one named last changes fastest.
Arguments:
- image: bfloat16 [8, 384, 2048], P('visit', None, 'sky'), may hold values from -16 to 16
- variance: bfloat16 [8, 384, 2048], P('visit', None, 'sky'), may hold values from 0.25 to 4
- mask_bits: int32 [8, 384, 2048], P('visit', None, 'sky'), may hold values from 0 to 63, as said below
- boxes: int32 [8, 4], P('visit'), may hold values from 0 to 2048, as said below
- row_filters: bfloat16 [20, 41], replicated, may hold values from -1 to 1
- col_filters: bfloat16 [20, 41], replicated, may hold values from -1 to 1
- coeffs: float32 [8, 20, 6], P('visit'), may hold values from -1.25 to 1.25
Outputs:
- coadd: float32 [384, 2048], P('visit', 'sky')
- weight_sum: float32 [384, 2048], P('visit', 'sky')
The draws below stay inside these ranges and needn't reach their ends.
Inputs may be any that keep to these rules, and one draw needn't show every extreme that they name: `mask_bits`: bits 0 to 5 may be set; bits 0, 1 and 2 reject a pixel. `boxes`: for every piece the first row is below the end row and the first column below the end column.
All inputs are finite; a program needn't handle non-finite values.
Results may differ from the reference program's by a relative error of at most 0.0029.
Values may be sent and summed in bfloat16 or wider, within the bound.
A program may use at most 64 MiB of HBM per device.

```python
import math
import jax
import jax.numpy as jnp
from jax import lax

RAD = 20
TAPS = 41
BASIS = 20
TERMS = 6
ROWS_DEV = 48
COLS_DEV = 512
PIECES = 8
H = 384
W = 2048
N_VISIT = 8


def draw_boxes(key, part):
    key_list = jax.random.split(key, 4)
    row_first = jax.random.randint(key_list[0], (PIECES,), 0, H // 4)
    row_end = H - jax.random.randint(key_list[1], (PIECES,), 0, H // 4)
    col_first = jax.random.randint(key_list[2], (PIECES,), 0, W // 4)
    col_end = W - jax.random.randint(key_list[3], (PIECES,), 0, W // 4)
    return jnp.stack([row_first, row_end, col_first, col_end], axis=1).astype(jnp.int32)


def draw_mask_bits(key, part):
    bit_sum = jnp.zeros((PIECES, H, W), jnp.int32)
    for bit_number in range(6):
        hit_mask = jax.random.randint(jax.random.fold_in(key, bit_number), (PIECES, H, W), 0, 16) == 0
        bit_sum = bit_sum + hit_mask.astype(jnp.int32) * 2 ** bit_number
    return bit_sum


def block_scale(own_key, extent, cuts, least, top_value):
    factor_of = 1.0
    for position, shards_of in cuts:
        steps = jax.random.uniform(jax.random.fold_in(jax.random.fold_in(own_key, 6), position), (shards_of,), jnp.float32, least / len(cuts), top_value / len(cuts))
        factor_of = factor_of * jnp.repeat(jnp.exp(steps), extent[position] // shards_of).reshape((-1,) + (1,) * (len(extent) - 1 - position))
    return factor_of


def scatter_about(own_key, extent, deviation, reach, shards=(), kind=jnp.bfloat16):
    level = block_scale(own_key, extent, shards, -0.22, 0.18) if shards else 1.0
    entries = jax.random.normal(own_key, extent, jnp.float32) * deviation * level
    return jnp.minimum(jnp.maximum(entries, -reach), reach).astype(kind)


def setup_inputs(seed: int = 0) -> dict:
    key_of = jax.random.split(jax.random.key(seed), 8)
    return {
        "image": scatter_about(key_of[0], (PIECES, H, W), 3.0, 16.0, ((0, 8), (2, 4))),
        "variance": jnp.clip(jnp.exp(math.log(4.0) - 2.7725887 * jax.random.uniform(key_of[1], (PIECES, H, W), jnp.float32) ** block_scale(key_of[1], (PIECES, H, W), ((0, 8), (2, 4)), -0.2, 0.2)), 0.25, 4.0).astype(jnp.bfloat16),
        "mask_bits": draw_mask_bits(jax.random.fold_in(key_of[7], 71), 0),
        "boxes": draw_boxes(jax.random.fold_in(key_of[7], 71), 0),
        "row_filters": scatter_about(key_of[4], (BASIS, TAPS), TAPS ** -0.5, 1.0),
        "col_filters": scatter_about(key_of[5], (BASIS, TAPS), TAPS ** -0.5, 1.0),
        "coeffs": scatter_about(key_of[6], (PIECES, BASIS, TERMS), BASIS ** -0.5, 1.25, ((0, 8),), jnp.float32),
    }


reject_bits = 7


def toeplitz_stack(filters, out_len, in_len):
    offsets = jnp.arange(in_len, dtype=jnp.int32)[None, :] - jnp.arange(out_len, dtype=jnp.int32)[:, None]
    onehot = (offsets[:, :, None] == jnp.arange(filters.shape[1], dtype=jnp.int32)[None, None, :]).astype(jnp.float32)
    return jnp.einsum("oit,bt->boi", onehot, filters.astype(jnp.float32), precision=lax.Precision.HIGHEST)


def reference(image, variance, mask_bits, boxes, row_filters, col_filters, coeffs):
    height = image.shape[1]
    width = image.shape[2]
    col_block = min(128, COLS_DEV)
    window_rows = ROWS_DEV + 2 * RAD
    row_mats = toeplitz_stack(row_filters, ROWS_DEV, window_rows)
    col_mats = toeplitz_stack(col_filters, col_block, col_block + 2 * RAD)
    row_index = jnp.arange(height, dtype=jnp.int32)[:, None]
    col_index = jnp.arange(width, dtype=jnp.int32)[None, :]
    ycoord = (2.0 * row_index.astype(jnp.float32) + 1.0) / height - 1.0
    xcoord = (2.0 * col_index.astype(jnp.float32) + 1.0) / width - 1.0
    count_blocks = width // col_block

    def one_piece(carry, items):
        picture, spread, bit_plane, piece_box, factors = items
        inside = (row_index >= piece_box[0]) & (row_index < piece_box[1])
        inside = inside & (col_index >= piece_box[2]) & (col_index < piece_box[3])
        inside = inside & (jnp.bitwise_and(bit_plane, reject_bits) == 0)
        masked = jnp.where(inside, spread, jnp.zeros_like(spread))
        positive = masked > 0
        weights = jnp.where(positive, 1.0 / jnp.where(positive, masked, jnp.ones_like(masked)).astype(jnp.float32), jnp.float32(0.0))
        extended = jnp.pad(picture, ((RAD, RAD), (RAD, RAD))).astype(jnp.float32)
        windows = jnp.stack([extended[:, block_id * col_block:block_id * col_block + col_block + 2 * RAD] for block_id in range(count_blocks)], axis=1)

        def basis_step(total, basis_items):
            col_mat, row_mat, poly_terms = basis_items
            colpass = jnp.einsum("rkj,cj->rkc", windows, col_mat, precision=lax.Precision.HIGHEST).astype(jnp.bfloat16)
            colpass = lax.optimization_barrier(colpass).astype(jnp.float32).reshape(height + 2 * RAD, width)
            bands = jnp.stack([colpass[band_id * ROWS_DEV:band_id * ROWS_DEV + window_rows] for band_id in range(N_VISIT)])
            rowpass = jnp.einsum("sr,vrc->vsc", row_mat, bands, precision=lax.Precision.HIGHEST).reshape(height, width)
            coef_field = poly_terms[0] + poly_terms[1] * xcoord + poly_terms[2] * ycoord + poly_terms[3] * (xcoord * xcoord) + poly_terms[4] * (xcoord * ycoord) + poly_terms[5] * (ycoord * ycoord)
            return total + coef_field * rowpass, None

        matched, _ = lax.scan(basis_step, jnp.zeros((height, width), jnp.float32), (col_mats, row_mats, factors))
        running_sum, weight_total = carry
        return (running_sum + weights * matched, weight_total + weights), None

    start_pair = (jnp.zeros((height, width), jnp.float32), jnp.zeros((height, width), jnp.float32))
    (numerator, denominator), _ = lax.scan(one_piece, start_pair, (image, variance, mask_bits, boxes, coeffs))
    return numerator / jnp.maximum(denominator, 1.0), denominator
```

```python
import functools

import jax
import jax.numpy as jnp
from jax import lax
from jax.experimental import pallas as pl
from jax.experimental.pallas import tpu as pltpu
from jax.sharding import PartitionSpec as P

RAD = 20
ROWS_DEV = 48
REJECT = 7
LANES = 128
CORES = 2
LEAD = 8
TOP = 24
WIN = 2 * ROWS_DEV
PACK = 5
TERMS = 6
MESH = pl.DeviceIdType.MESH


def weight_of(plane):
    plane = plane.astype(jnp.float32)
    positive = plane > 0
    return jnp.where(positive, 1.0 / jnp.where(positive, plane, 1.0), 0.0)


def kernel(
    visits,
    skies,
    image_hbm,
    var_hbm,
    bits_hbm,
    boxes_hbm,
    rowf_hbm,
    colf_hbm,
    coef_hbm,
    sums_ref,
    image_ref,
    var_ref,
    bits_ref,
    boxes_ref,
    rowf_ref,
    colf_ref,
    coef_ref,
    edge_send,
    edge_got,
    wide,
    masked,
    sib_var,
    pair_w,
    got_w,
    own_pix,
    sib_send,
    sib_pix,
    pair_pix,
    got_pix,
    filt,
    col_mats,
    passed,
    toeplitz,
    factors,
    row_mats,
    row_last,
    load_sem,
    halo_send,
    halo_recv,
    var_send,
    var_recv,
    w_send,
    w_recv,
    sib_send_sem,
    sib_recv_sem,
    pix_send,
    pix_recv,
):
    height, cols = var_ref.shape[1], var_ref.shape[2]
    width = cols * skies
    basis, taps = rowf_ref.shape
    blocks = cols // LANES
    inner, outer = list(range(1, blocks - 1)), [0, blocks - 1]
    chips = visits // CORES
    few = chips == 4
    deep = basis * WIN
    f32, bf16 = jnp.float32, jnp.bfloat16
    v = lax.axis_index("visit")
    z = lax.axis_index("sky")
    chip = v // CORES
    core = lax.rem(v, CORES)
    sibling = chip * CORES + 1 - core
    has_l = z > 0
    has_r = z < skies - 1

    def chip_at(slot):
        if not few:
            return lax.rem(chip + slot + 1, chips)
        return [chips - 1 - chip, lax.rem(chip + 2, chips), chip + 1 - 2 * lax.rem(chip, 2), chip][slot]

    def each(first, last, body):
        if few:
            for slot in range(first, last):
                body(slot)
        else:

            def one(slot, carry):
                body(slot)
                return carry

            lax.fori_loop(first, last, one, 0)

    barrier = pltpu.get_barrier_semaphore()
    pl.semaphore_signal(barrier, inc=1, device_id=(sibling, z), device_id_type=MESH)
    for slot in range(chips - 1):
        pl.semaphore_signal(
            barrier, inc=1, device_id=(chip_at(slot) * CORES + core, z), device_id_type=MESH
        )

    @pl.when(has_l)
    def _():
        pl.semaphore_signal(barrier, inc=1, device_id=(v, z - 1), device_id_type=MESH)

    @pl.when(has_r)
    def _():
        pl.semaphore_signal(barrier, inc=1, device_id=(v, z + 1), device_id_type=MESH)

    pairs = (
        (image_hbm.at[0], image_ref.at[pl.ds(16, height)]),
        (rowf_hbm, rowf_ref),
        (colf_hbm, colf_ref),
        (coef_hbm, coef_ref),
        (boxes_hbm, boxes_ref),
        (var_hbm, var_ref),
        (bits_hbm, bits_ref),
    )
    loads = [
        pltpu.make_async_copy(src, dst, load_sem.at[n]) for n, (src, dst) in enumerate(pairs)
    ]
    for load in loads:
        load.start()

    below = image_ref.shape[0] - 16 - height
    image_ref[0:16, :] = jnp.zeros((16, cols), bf16)
    image_ref[16 + height :, :] = jnp.zeros((below, cols), bf16)
    for b in range(basis):
        passed[b, 0:16, :] = jnp.zeros((16, cols), bf16)
        passed[b, height + 32 : height + 48, :] = jnp.zeros((16, cols), bf16)

    for load in loads[1:4]:
        load.wait()
    filt[...] = jnp.zeros_like(filt)
    filt[0:basis, 0:taps] = colf_ref[...].astype(f32)

    def build(b):
        col = jnp.broadcast_to(filt[pl.ds(b, 1), :], (LANES, 2 * LANES))
        col_mats[b] = pltpu.roll(col, 0, 1, stride=1, stride_axis=0).astype(bf16)

    col_first = z * cols
    group_of = lax.broadcasted_iota(jnp.int32, (1, deep), 1) // WIN
    tap_of = lax.broadcasted_iota(jnp.int32, (1, deep), 1) - group_of * WIN - (TOP - RAD)
    tap_mat = (lax.broadcasted_iota(jnp.int32, (taps, deep), 0) == tap_of).astype(f32).astype(bf16)
    own_group = (lax.broadcasted_iota(jnp.int32, (basis, deep), 0) == group_of).astype(f32)
    every = jnp.dot(rowf_ref[...], tap_mat, preferred_element_type=f32)
    line = jnp.sum(every * own_group, axis=0, keepdims=True)
    toeplitz[...] = pltpu.roll(
        jnp.broadcast_to(line, (ROWS_DEV, deep)), 0, 1, stride=1, stride_axis=0
    )
    c = jnp.dot(
        coef_ref[:, 0, :], own_group, precision=lax.Precision.HIGHEST, preferred_element_type=f32
    )
    c = [c[t : t + 1] for t in range(TERMS)]
    xc = (2 * col_first + cols).astype(f32) / width - 1.0
    factors[0:1] = c[0] + xc * (c[1] + xc * c[3])
    factors[1:2] = c[2] + xc * c[4]
    factors[2:3] = c[5]
    factors[3:4] = c[1] + (2.0 * xc) * c[3]
    factors[4:5] = c[4]
    row_last[...] = (toeplitz[...] * c[3]).astype(bf16)
    y_iota = lax.broadcasted_iota(jnp.int32, (ROWS_DEV, LANES), 0)
    tiles = deep // LANES

    def build_rows(band, at, first, last, tie):
        y = (2.0 * (band * ROWS_DEV + y_iota).astype(f32) + 1.0) / height - 1.0 + tie
        for n in range(first, last):
            lanes = slice(n * LANES, (n + 1) * LANES)
            base = toeplitz[:, lanes]
            f = [factors[t : t + 1, lanes] for t in range(5)]
            row_mats[at, 0:ROWS_DEV, lanes] = (base * (f[0] + y * (f[1] + y * f[2]))).astype(bf16)
            row_mats[at, ROWS_DEV : 2 * ROWS_DEV, lanes] = (base * (f[3] + y * f[4])).astype(bf16)

    lane = lax.broadcasted_iota(jnp.int32, (1, LANES), 1)
    strip = wide.shape[0] // PACK
    loads[0].wait()
    to_l = to_r = jnp.zeros((strip, LANES), f32)
    for g in range(PACK):
        rows = slice(g * strip, (g + 1) * strip)
        part = image_ref[g * strip : (g + 1) * strip + 16, :].astype(f32)[LEAD : LEAD + strip]
        part = pltpu.roll(part, RAD, 1)
        wide[rows, LANES:cols] = part[:, LANES:].astype(bf16)
        edge = part[:, :LANES]
        wide[rows, cols:] = edge.astype(bf16)
        at = g * RAD
        edge = pltpu.roll(edge, at, 1) if g else edge
        to_r = jnp.where((lane >= at) & (lane < at + RAD), edge, to_r)
        to_l = jnp.where((lane >= at + RAD) & (lane < at + 2 * RAD), edge, to_l)
    edge_send[0] = to_l.astype(bf16)
    edge_send[1] = to_r.astype(bf16)

    for load in loads[4:]:
        load.wait()
    box = [boxes_ref[0, i] for i in range(4)]
    col_index = col_first + lax.broadcasted_iota(jnp.int32, (ROWS_DEV, cols), 1)
    col_inside = (col_index >= box[2]) & (col_index < box[3])
    row_iota = lax.broadcasted_iota(jnp.int32, (ROWS_DEV, cols), 0)

    def mask_band(band, carry):
        first = pl.multiple_of(band * ROWS_DEV, ROWS_DEV)
        rows = pl.ds(first, ROWS_DEV)
        row_index = first + row_iota
        inside = (row_index >= box[0]) & (row_index < box[1]) & col_inside
        inside = inside & ((bits_ref[0, rows, :] & REJECT) == 0)
        masked[lax.rem(band, CORES), band // CORES] = jnp.where(
            inside, var_ref[0, rows, :].astype(f32), 0.0
        ).astype(bf16)
        return carry

    lax.fori_loop(0, visits, mask_band, 0, unroll=few)

    pl.semaphore_wait(barrier, chips + has_l.astype(jnp.int32) + has_r.astype(jnp.int32))

    def remote(src, dst, send, recv, target):
        return pltpu.make_async_remote_copy(
            src_ref=src,
            dst_ref=dst,
            send_sem=send,
            recv_sem=recv,
            device_id=target,
            device_id_type=MESH,
        )

    def edge_copy(side, target):
        return remote(
            edge_send.at[side],
            edge_got.at[side],
            halo_send.at[side],
            halo_recv.at[side],
            (v, target),
        )

    def peer(slot):
        return (chip_at(slot) * CORES + core, z)

    def var_copy():
        return remote(
            masked.at[1 - core], sib_var, var_send.at[0], var_recv.at[0], (sibling, z)
        )

    def w_copy(slot):
        return remote(
            pair_w.at[slot], got_w.at[slot], w_send.at[slot], w_recv.at[slot], peer(slot)
        )

    def sib_copy(slot):
        return remote(
            sib_send.at[slot],
            sib_pix.at[slot],
            sib_send_sem.at[slot],
            sib_recv_sem.at[slot],
            (sibling, z),
        )

    def pix_copy(slot):
        return remote(
            pair_pix.at[slot], got_pix.at[slot], pix_send.at[slot], pix_recv.at[slot], peer(slot)
        )

    @pl.when(has_l)
    def _():
        edge_copy(0, z - 1).start()

    @pl.when(has_r)
    def _():
        edge_copy(1, z + 1).start()

    var_copy().start()

    def col_step(p, first, rows, which):
        parts = [wide[pl.ds(first, rows), k * LANES : (k + 2) * LANES] for k in which]
        mats = col_mats[pl.ds(2 * p, 2)].reshape(2 * LANES, 2 * LANES)
        out = lax.dot_general(
            jnp.concatenate(parts, axis=0),
            mats,
            (((1,), (1,)), ((), ())),
            preferred_element_type=f32,
        )
        into = pl.ds(pl.multiple_of(first + 16, 16), rows)
        for n, k in enumerate(which):
            for h in range(2):
                passed[2 * p + h, into, k * LANES : (k + 1) * LANES] = out[
                    n * rows : (n + 1) * rows, h * LANES : (h + 1) * LANES
                ].astype(bf16)
        return out[0:1, 0:LANES] * 0.0

    def weighted(slot, side, at):
        at_chip = chip_at(slot)
        band = at_chip * CORES + side
        if not few:
            build_rows(band, at, 0, tiles, 0.0)
        rows = pl.ds(pl.multiple_of(band * ROWS_DEV, 16), WIN)
        mats = jnp.concatenate([row_mats[at], row_last[...]], axis=0)
        out = jnp.dot(mats, passed[:, rows, :].reshape(deep, cols), preferred_element_type=f32)
        x = (2 * lax.broadcasted_iota(jnp.int32, (1, cols), 1) + 1 - cols).astype(f32) / width
        pixels = out[0:ROWS_DEV] + x * (
            out[ROWS_DEV : 2 * ROWS_DEV] + x * out[2 * ROWS_DEV : 3 * ROWS_DEV]
        )
        return pixels * weight_of(masked[side, at_chip])

    def for_sibling(slot, at=0):
        sib_send[slot] = weighted(slot, 1 - core, at)

    def for_own(slot, at=0):
        own_pix[slot] = weighted(slot, core, at)

    def send_pair(slot):
        sib_copy(slot).wait_recv()
        pair_pix[slot] = (own_pix[slot] + sib_pix[slot]).astype(bf16)
        pix_copy(slot).start()

    def pair_weight(slot):
        at_chip = chip_at(slot)
        return weight_of(masked[core, at_chip]) + weight_of(sib_var[at_chip])

    def send_weight(slot):
        pair_w[slot] = pair_weight(slot).astype(bf16)
        w_copy(slot).start()

    def edges():
        @pl.when(has_l)
        def _():
            edge_copy(1, z - 1).wait_recv()

        @pl.when(has_r)
        def _():
            edge_copy(0, z + 1).wait_recv()

        @pl.when(jnp.logical_not(has_l))
        def _():
            edge_got[1] = jnp.zeros((strip, LANES), bf16)

        @pl.when(jnp.logical_not(has_r))
        def _():
            edge_got[0] = jnp.zeros((strip, LANES), bf16)

        for g in range(PACK):
            rows = slice(g * strip, (g + 1) * strip)
            mine = wide[rows, cols:].astype(f32)
            from_r, from_l = (edge_got[side].astype(f32) for side in range(2))
            if g:
                from_r = pltpu.roll(from_r, LANES - g * RAD, 1)
                from_l = pltpu.roll(from_l, LANES - g * RAD, 1)
            wide[rows, 0:LANES] = jnp.where(lane < RAD, from_l, mine).astype(bf16)
            wide[rows, cols:] = jnp.where(
                (lane >= RAD) & (lane < 2 * RAD), from_r, mine
            ).astype(bf16)

    def own_sums():
        sums_ref[1] = pair_weight(chips - 1)

    def add_weight(slot):
        w_copy(slot).wait_recv()
        sums_ref[1] += got_w[slot].astype(f32)

    def add_own():
        sib_copy(chips - 1).wait_recv()
        sums_ref[0] = own_pix[chips - 1] + sib_pix[chips - 1]

    def add_pixels(slot):
        pix_copy(slot).wait_recv()
        sums_ref[0] += got_pix[slot].astype(f32)

    steps = basis // 2
    if few:
        half = chips // 2 * CORES * ROWS_DEV
        group = chip // 2
        total = height + 2 * LEAD
        early = half + 2 * LEAD + LEAD * 2
        far = pl.multiple_of((1 - group) * (total - early), 16)
        near = pl.multiple_of(group * early, 16)
        bands = [(0, 1), (1, 1), (0, 0), (1, 0), (2, 1), (2, 0), (3, 1), (3, 0)]

        def band_of(at):
            slot, other = bands[at]
            return chip_at(slot) * CORES + (1 - core if other else core)

        def columns(first, rows, which, base, share, build_too=False):
            for p in range(steps):
                if build_too:
                    build(2 * p)
                    build(2 * p + 1)
                tie = col_step(p, first, rows, which)
                n = 3 * (p % share)
                build_rows(band_of(base + p // share), base + p // share, n, n + tiles // share, tie)

        share = 5
        columns(far, early, inner, 0, share, True)
        edges()
        var_copy().wait_recv()
        for slot in range(chips - 1):
            send_weight(slot)
        columns(far, early, outer, 2, share)
        for_sibling(0, 0)
        for_sibling(1, 1)
        sib_copy(0).start()
        sib_copy(1).start()
        for_own(0, 2)
        for_own(1, 3)
        columns(near, total - early, inner, 4, share)
        send_pair(0)
        send_pair(1)
        columns(near, total - early, outer, 6, share)
        for_sibling(2, 4)
        sib_copy(2).start()
        for_own(2, 5)
        for_sibling(3, 6)
        sib_copy(3).start()
        own_sums()
        for slot in range(chips - 1):
            add_weight(slot)
        for_own(3, 7)
        send_pair(2)
    else:
        edges()

        def one(p, carry):
            build(2 * p)
            build(2 * p + 1)
            for k in range(blocks):
                col_step(p, 0, height + 2 * LEAD, [k])
            return carry

        lax.fori_loop(0, steps, one, 0)
        var_copy().wait_recv()
        each(0, chips - 1, send_weight)

        def sibling_band(slot):
            for_sibling(slot)
            sib_copy(slot).start()

        each(0, chips, sibling_band)
        each(0, chips, for_own)
        each(0, chips - 1, send_pair)
        own_sums()
        each(0, chips - 1, add_weight)

    add_own()
    each(0, chips - 1, add_pixels)

    var_copy().wait_send()

    def drain(slot):
        w_copy(slot).wait_send()
        pix_copy(slot).wait_send()

    each(0, chips - 1, drain)
    each(0, chips, lambda slot: sib_copy(slot).wait_send())

    @pl.when(has_l)
    def _():
        edge_copy(0, z - 1).wait_send()

    @pl.when(has_r)
    def _():
        edge_copy(1, z + 1).wait_send()


def per_device(image, variance, mask_bits, boxes, row_filters, col_filters, coeffs):
    height, cols = image.shape[1], image.shape[2]
    visits, skies = lax.axis_size("visit"), lax.axis_size("sky")
    basis = row_filters.shape[0]
    chips = visits // CORES
    few = chips == 4
    deep = basis * WIN
    unit = 16 * PACK
    tall = (height + 2 * LEAD + unit - 1) // unit * unit
    coeffs = jnp.transpose(coeffs, (2, 0, 1))
    hbm = pl.BlockSpec(memory_space=pltpu.HBM)
    f32, bf16 = jnp.float32, jnp.bfloat16
    dma = pltpu.SemaphoreType.DMA
    sums = pl.pallas_call(
        functools.partial(kernel, visits, skies),
        out_shape=jax.ShapeDtypeStruct((2, ROWS_DEV, cols), f32),
        in_specs=[hbm] * 7,
        out_specs=pl.BlockSpec(memory_space=pltpu.VMEM),
        scratch_shapes=[
            pltpu.VMEM((tall + 16, cols), bf16),
            pltpu.VMEM(variance.shape, bf16),
            pltpu.VMEM(mask_bits.shape, jnp.int32),
            pltpu.SMEM(boxes.shape, jnp.int32),
            pltpu.VMEM(row_filters.shape, bf16),
            pltpu.VMEM(col_filters.shape, bf16),
            pltpu.VMEM(coeffs.shape, f32),
            pltpu.VMEM((2, tall // PACK, LANES), bf16),
            pltpu.VMEM((2, tall // PACK, LANES), bf16),
            pltpu.VMEM((tall, cols + LANES), bf16),
            pltpu.VMEM((CORES, chips, ROWS_DEV, cols), bf16),
            pltpu.VMEM((chips, ROWS_DEV, cols), bf16),
            pltpu.VMEM((chips, ROWS_DEV, cols), bf16),
            pltpu.VMEM((chips, ROWS_DEV, cols), bf16),
            pltpu.VMEM((chips, ROWS_DEV, cols), f32),
            pltpu.VMEM((chips, ROWS_DEV, cols), f32),
            pltpu.VMEM((chips, ROWS_DEV, cols), f32),
            pltpu.VMEM((chips, ROWS_DEV, cols), bf16),
            pltpu.VMEM((chips, ROWS_DEV, cols), bf16),
            pltpu.VMEM((24, 2 * LANES), f32),
            pltpu.VMEM((basis, LANES, 2 * LANES), bf16),
            pltpu.VMEM((basis, height + 2 * TOP, cols), bf16),
            pltpu.VMEM((ROWS_DEV, deep), f32),
            pltpu.VMEM((8, deep), f32),
            pltpu.VMEM((visits if few else 1, 2 * ROWS_DEV, deep), bf16),
            pltpu.VMEM((ROWS_DEV, deep), bf16),
            dma((7,)),
            dma((2,)),
            dma((2,)),
            dma((1,)),
            dma((1,)),
            dma((chips,)),
            dma((chips,)),
            dma((chips,)),
            dma((chips,)),
            dma((chips,)),
            dma((chips,)),
        ],
        compiler_params=pltpu.CompilerParams(
            collective_id=0, has_side_effects=True, vmem_limit_bytes=62 * 1024 * 1024
        ),
    )(image, variance, mask_bits, boxes, row_filters, col_filters, coeffs)
    return (sums[0] / jnp.maximum(sums[1], 1.0), sums[1])


def solution(mesh):
    in_specs = (
        P("visit", None, "sky"),
        P("visit", None, "sky"),
        P("visit", None, "sky"),
        P("visit", None),
        P(),
        P(),
        P("visit", None, None),
    )
    out_specs = (P("visit", "sky"), P("visit", "sky"))
    return jax.shard_map(
        per_device, mesh=mesh, in_specs=in_specs, out_specs=out_specs, check_vma=False
    )
```

```python
import functools

import jax
import jax.numpy as jnp
from jax import lax
from jax.experimental import pallas as pl
from jax.experimental.pallas import tpu as pltpu
from jax.sharding import PartitionSpec as P

RAD = 20
ROWS_DEV = 48
REJECT = 7
LANES = 128
CORES = 2
LEAD = 8
TOP = 24
WIN = 2 * ROWS_DEV
PACK = 5
TERMS = 6
MESH = pl.DeviceIdType.MESH


def weight_of(plane):
    plane = plane.astype(jnp.float32)
    positive = plane > 0
    return jnp.where(positive, 1.0 / jnp.where(positive, plane, 1.0), 0.0)


def kernel(
    visits,
    skies,
    image_hbm,
    var_hbm,
    bits_hbm,
    boxes_hbm,
    rowf_hbm,
    colf_hbm,
    coef_hbm,
    sums_ref,
    image_ref,
    var_ref,
    bits_ref,
    boxes_ref,
    rowf_ref,
    colf_ref,
    coef_ref,
    edge_send,
    edge_got,
    wide,
    masked,
    got_var,
    own_pix,
    sib_send,
    sib_pix,
    pair_pix,
    got_pix,
    filt,
    col_mats,
    passed,
    toeplitz,
    factors,
    row_mats,
    row_last,
    load_sem,
    halo_send,
    halo_recv,
    var_send,
    var_recv,
    sib_send_sem,
    sib_recv_sem,
    pix_send,
    pix_recv,
):
    height, cols = var_ref.shape[1], var_ref.shape[2]
    width = cols * skies
    basis, taps = rowf_ref.shape
    blocks = cols // LANES
    inner, outer = list(range(1, blocks - 1)), [0, blocks - 1]
    chips = visits // CORES
    few = chips == 4
    deep = basis * WIN
    f32, bf16 = jnp.float32, jnp.bfloat16
    v = lax.axis_index("visit")
    z = lax.axis_index("sky")
    chip = v // CORES
    core = lax.rem(v, CORES)
    sibling = chip * CORES + 1 - core
    has_l = z > 0
    has_r = z < skies - 1

    def chip_at(slot):
        if not few:
            return lax.rem(chip + slot + 1, chips)
        return [chips - 1 - chip, lax.rem(chip + 2, chips), chip + 1 - 2 * lax.rem(chip, 2), chip][slot]

    def each(first, last, body):
        if few:
            for slot in range(first, last):
                body(slot)
        else:

            def one(slot, carry):
                body(slot)
                return carry

            lax.fori_loop(first, last, one, 0)

    barrier = pltpu.get_barrier_semaphore()
    for step in range(1, visits):
        pl.semaphore_signal(
            barrier, inc=1, device_id=(lax.rem(v + step, visits), z), device_id_type=MESH
        )

    @pl.when(has_l)
    def _():
        pl.semaphore_signal(barrier, inc=1, device_id=(v, z - 1), device_id_type=MESH)

    @pl.when(has_r)
    def _():
        pl.semaphore_signal(barrier, inc=1, device_id=(v, z + 1), device_id_type=MESH)

    pairs = (
        (rowf_hbm, rowf_ref),
        (colf_hbm, colf_ref),
        (coef_hbm, coef_ref),
        (image_hbm.at[0], image_ref.at[pl.ds(16, height)]),
        (boxes_hbm, boxes_ref),
        (var_hbm, var_ref),
        (bits_hbm, bits_ref),
    )
    loads = [
        pltpu.make_async_copy(src, dst, load_sem.at[n]) for n, (src, dst) in enumerate(pairs)
    ]
    for load in loads:
        load.start()

    below = image_ref.shape[0] - 16 - height
    image_ref[0:16, :] = jnp.zeros((16, cols), bf16)
    image_ref[16 + height :, :] = jnp.zeros((below, cols), bf16)
    col_first = z * cols
    for pair in passed:
        for h in range(2):
            pair[h, 0:16, :] = jnp.zeros((16, cols), bf16)
            pair[h, pair.shape[1] - 16 :, :] = jnp.zeros((16, cols), bf16)

    for load in loads[:3]:
        load.wait()
    filt[...] = jnp.zeros_like(filt)
    filt[0:basis, 0:taps] = colf_ref[...].astype(f32)
    lane = lax.broadcasted_iota(jnp.int32, (1, LANES), 1)
    ahead = lax.broadcasted_iota(jnp.int32, (LANES, LANES), 1) >= lax.broadcasted_iota(
        jnp.int32, (LANES, LANES), 0
    )

    def build(b):
        col = jnp.broadcast_to(filt[pl.ds(b, 1), :], (LANES, LANES))
        col = pltpu.roll(col, 0, 1, stride=1, stride_axis=0)
        col_mats[b, :, 0:LANES] = jnp.where(ahead, col, 0.0).astype(bf16)
        col_mats[b, :, LANES : 2 * LANES] = jnp.where(ahead, 0.0, col).astype(bf16)

    group_of = lax.broadcasted_iota(jnp.int32, (1, deep), 1) // WIN
    tap_of = lax.broadcasted_iota(jnp.int32, (1, deep), 1) - group_of * WIN - (TOP - RAD)
    tap_mat = (lax.broadcasted_iota(jnp.int32, (taps, deep), 0) == tap_of).astype(f32).astype(bf16)
    own_group = (lax.broadcasted_iota(jnp.int32, (basis, deep), 0) == group_of).astype(f32)
    every = jnp.dot(rowf_ref[...], tap_mat, preferred_element_type=f32)
    line = jnp.sum(every * own_group, axis=0, keepdims=True)
    toeplitz[...] = pltpu.roll(
        jnp.broadcast_to(line, (ROWS_DEV, deep)), 0, 1, stride=1, stride_axis=0
    )
    c = jnp.dot(
        coef_ref[:, 0, :], own_group, precision=lax.Precision.HIGHEST, preferred_element_type=f32
    )
    c = [c[t : t + 1] for t in range(TERMS)]
    xc = (2 * col_first + cols).astype(f32) / width - 1.0
    factors[0:1] = c[0] + xc * (c[1] + xc * c[3])
    factors[1:2] = c[2] + xc * c[4]
    factors[2:3] = c[5]
    factors[3:4] = c[1] + (2.0 * xc) * c[3]
    factors[4:5] = c[4]
    row_last[...] = (toeplitz[...] * c[3]).astype(bf16)
    y_iota = lax.broadcasted_iota(jnp.int32, (ROWS_DEV, LANES), 0)
    tiles = deep // LANES

    def build_rows(band, at, first, last, tie):
        y = (2.0 * (band * ROWS_DEV + y_iota).astype(f32) + 1.0) / height - 1.0 + tie
        for n in range(first, last):
            lanes = slice(n * LANES, (n + 1) * LANES)
            base = toeplitz[:, lanes]
            f = [factors[t : t + 1, lanes] for t in range(5)]
            row_mats[at][0:ROWS_DEV, lanes] = (base * (f[0] + y * (f[1] + y * f[2]))).astype(bf16)
            row_mats[at][ROWS_DEV : 2 * ROWS_DEV, lanes] = (base * (f[3] + y * f[4])).astype(bf16)

    strip = wide.shape[0] // PACK
    loads[3].wait()
    to_l = to_r = jnp.zeros((strip, LANES), f32)
    for g in range(PACK):
        rows = slice(g * strip, (g + 1) * strip)
        part = image_ref[g * strip : (g + 1) * strip + 16, :].astype(f32)[LEAD : LEAD + strip]
        part = pltpu.roll(part, RAD, 1)
        wide[rows, LANES:cols] = part[:, LANES:].astype(bf16)
        edge = part[:, :LANES]
        wide[rows, cols:] = edge.astype(bf16)
        at = g * RAD
        edge = pltpu.roll(edge, at, 1) if g else edge
        to_r = jnp.where((lane >= at) & (lane < at + RAD), edge, to_r)
        to_l = jnp.where((lane >= at + RAD) & (lane < at + 2 * RAD), edge, to_l)
    edge_send[0] = to_l.astype(bf16)
    edge_send[1] = to_r.astype(bf16)

    def remote(src, dst, send, recv, target):
        return pltpu.make_async_remote_copy(
            src_ref=src,
            dst_ref=dst,
            send_sem=send,
            recv_sem=recv,
            device_id=target,
            device_id_type=MESH,
        )

    def edge_copy(side, target):
        return remote(
            edge_send.at[side],
            edge_got.at[side],
            halo_send.at[side],
            halo_recv.at[side],
            (v, target),
        )

    def peer(slot):
        return (chip_at(slot) * CORES + core, z)

    def var_copy(slot, other):
        side = 1 - core if other else core
        return remote(
            masked.at[side, chip_at(slot)],
            got_var.at[slot, other],
            var_send.at[slot, other],
            var_recv.at[slot, other],
            (chip_at(slot) * CORES + side, z),
        )

    def for_vars(act):
        def both(slot):
            act(slot, 0)
            act(slot, 1)

        each(0, chips - 1, both)
        act(chips - 1, 1)

    def sib_copy(slot):
        return remote(
            sib_send.at[slot],
            sib_pix.at[slot],
            sib_send_sem.at[slot],
            sib_recv_sem.at[slot],
            (sibling, z),
        )

    def pix_copy(slot):
        return remote(
            pair_pix.at[slot], got_pix.at[slot], pix_send.at[slot], pix_recv.at[slot], peer(slot)
        )

    pl.semaphore_wait(barrier, visits - 1 + has_l.astype(jnp.int32) + has_r.astype(jnp.int32))

    @pl.when(has_l)
    def _():
        edge_copy(0, z - 1).start()

    @pl.when(has_r)
    def _():
        edge_copy(1, z + 1).start()

    for load in loads[4:]:
        load.wait()
    box = [boxes_ref[0, i] for i in range(4)]
    col_index = col_first + lax.broadcasted_iota(jnp.int32, (ROWS_DEV, cols), 1)
    col_inside = (col_index >= box[2]) & (col_index < box[3])
    row_iota = lax.broadcasted_iota(jnp.int32, (ROWS_DEV, cols), 0)

    def mask_band(band, carry):
        first = pl.multiple_of(band * ROWS_DEV, ROWS_DEV)
        rows = pl.ds(first, ROWS_DEV)
        row_index = first + row_iota
        inside = (row_index >= box[0]) & (row_index < box[1]) & col_inside
        inside = inside & ((bits_ref[0, rows, :] & REJECT) == 0)
        masked[lax.rem(band, CORES), band // CORES] = jnp.where(
            inside, var_ref[0, rows, :].astype(f32), 0.0
        ).astype(bf16)
        return carry

    lax.fori_loop(0, visits, mask_band, 0, unroll=few)
    for_vars(lambda slot, other: var_copy(slot, other).start())

    def col_step(p, first, rows, which):
        parts = [wide[pl.ds(first, rows), k * LANES : (k + 2) * LANES] for k in which]
        mats = col_mats[pl.ds(2 * p, 2)].reshape(2 * LANES, 2 * LANES)
        out = lax.dot_general(
            jnp.concatenate(parts, axis=0),
            mats,
            (((1,), (1,)), ((), ())),
            preferred_element_type=f32,
        )
        into = pl.ds(pl.multiple_of(first + 16, 16), rows)
        for n, k in enumerate(which):
            for h in range(2):
                passed[p][h, into, k * LANES : (k + 1) * LANES] = out[
                    n * rows : (n + 1) * rows, h * LANES : (h + 1) * LANES
                ].astype(bf16)
        return out[0:1, 0:LANES] * 0.0

    def picked(plane, which):
        if len(which) == blocks:
            return plane
        return jnp.concatenate([plane[..., k * LANES : (k + 1) * LANES] for k in which], axis=-1)

    def weighted(slot, side, at, which):
        at_chip = chip_at(slot)
        band = at_chip * CORES + side
        if not few:
            build_rows(band, at, 0, tiles, 0.0)
        rows = pl.ds(pl.multiple_of(band * ROWS_DEV, 16), WIN)
        mats = jnp.concatenate([row_mats[at][...], row_last[...]], axis=0)
        lines = jnp.concatenate(
            [
                jnp.concatenate(
                    [
                        pair[:, rows, k * LANES : (k + 1) * LANES].reshape(2 * WIN, LANES)
                        for pair in passed
                    ],
                    axis=0,
                )
                for k in which
            ],
            axis=1,
        )
        out = jnp.dot(mats, lines, preferred_element_type=f32)
        x = (2 * lax.broadcasted_iota(jnp.int32, (1, cols), 1) + 1 - cols).astype(f32) / width
        x = picked(x, which)
        pixels = out[0:ROWS_DEV] + x * (
            out[ROWS_DEV : 2 * ROWS_DEV] + x * out[2 * ROWS_DEV : 3 * ROWS_DEV]
        )
        return pixels * weight_of(picked(masked[side, at_chip], which)), out[0:1, 0:LANES] * 0.0

    def put(ref, slot, side, at, which):
        result, tie = weighted(slot, side, at, which)
        for n, k in enumerate(which):
            ref[slot, :, k * LANES : (k + 1) * LANES] = result[:, n * LANES : (n + 1) * LANES]
        return tie

    every_block = list(range(blocks))

    def for_sibling(slot, at=0, which=every_block):
        return put(sib_send, slot, 1 - core, at, which)

    def for_own(slot, at=0, which=every_block):
        return put(own_pix, slot, core, at, which)

    def send_pair(slot):
        sib_copy(slot).wait_recv()
        pair_pix[slot] = (own_pix[slot] + sib_pix[slot]).astype(bf16)
        pix_copy(slot).start()

    def edges():
        @pl.when(has_l)
        def _():
            edge_copy(1, z - 1).wait_recv()

        @pl.when(has_r)
        def _():
            edge_copy(0, z + 1).wait_recv()

        @pl.when(jnp.logical_not(has_l))
        def _():
            edge_got[1] = jnp.zeros((strip, LANES), bf16)

        @pl.when(jnp.logical_not(has_r))
        def _():
            edge_got[0] = jnp.zeros((strip, LANES), bf16)

    def merge_edges():
        for g in range(PACK):
            rows = slice(g * strip, (g + 1) * strip)
            mine = wide[rows, cols:].astype(f32)
            from_r, from_l = (edge_got[side].astype(f32) for side in range(2))
            if g:
                from_r = pltpu.roll(from_r, LANES - g * RAD, 1)
                from_l = pltpu.roll(from_l, LANES - g * RAD, 1)
            wide[rows, 0:LANES] = jnp.where(lane < RAD, from_l, mine).astype(bf16)
            wide[rows, cols:] = jnp.where(
                (lane >= RAD) & (lane < 2 * RAD), from_r, mine
            ).astype(bf16)

    def add_weights():
        sums_ref[1] = weight_of(masked[core, chip])

        def one(slot, other):
            var_copy(slot, other).wait_recv()
            sums_ref[1] += weight_of(got_var[slot, other])

        for_vars(one)

    def add_own():
        sib_copy(chips - 1).wait_recv()
        sums_ref[0] = own_pix[chips - 1] + sib_pix[chips - 1]

    def add_pixels(slot):
        pix_copy(slot).wait_recv()
        sums_ref[0] += got_pix[slot].astype(f32)

    steps = basis // 2
    if few:
        half = chips // 2 * CORES * ROWS_DEV
        group = chip // 2
        total = height + 2 * LEAD
        early = half + 2 * LEAD + LEAD * 2
        far = pl.multiple_of((1 - group) * (total - early), 16)
        near = pl.multiple_of(group * early, 16)
        bands = [(0, 1), (1, 1), (0, 0), (1, 0), (2, 1), (2, 0), (3, 1), (3, 0)]

        def band_of(at):
            slot, other = bands[at]
            return chip_at(slot) * CORES + (1 - core if other else core)

        def columns(first, rows, which, base, count, build_too=False):
            pieces = [(base + n // tiles, n % tiles) for n in range(count * tiles)]
            each_step = -(-len(pieces) // steps)
            for p in range(steps):
                if build_too:
                    build(2 * p)
                    build(2 * p + 1)
                tie = col_step(p, first, rows, which)
                mine = pieces[p * each_step : (p + 1) * each_step]
                for at in sorted({at for at, _ in mine}):
                    of = [n for a, n in mine if a == at]
                    build_rows(band_of(at), at, of[0], of[-1] + 1, tie)

        columns(far, early, inner, 0, 3, True)
        tie = for_sibling(0, 0, inner)
        build_rows(band_of(3), 3, 0, tiles, tie)
        for_sibling(1, 1, inner)
        edges()
        merge_edges()
        for_own(0, 2, inner)
        for_own(1, 3, inner)
        columns(far, early, outer, 4, 2)
        for slot in range(2):
            for_sibling(slot, slot, outer)
        for slot in range(2):
            for_own(slot, 2 + slot, outer)
        for slot in range(2):
            sib_copy(slot).start()
        columns(near, total - early, inner, 6, 1)
        columns(near, total - early, outer, 7, 1)
        for_sibling(2, 4)
        sib_copy(2).start()
        send_pair(0)
        send_pair(1)
        for_own(2, 5)
        for_sibling(3, 6)
        for_own(3, 7)
        sib_copy(3).start()
        send_pair(2)
    else:
        edges()
        merge_edges()
        for b in range(basis):
            build(b)

        def one(g, carry):
            for p in range(steps):
                for which in (inner, outer):
                    col_step(p, pl.multiple_of(g * strip, 16), strip, which)
            return carry

        lax.fori_loop(0, PACK, one, 0)

        def sibling_band(slot):
            for_sibling(slot)
            sib_copy(slot).start()

        each(0, chips, sibling_band)
        each(0, chips, for_own)
        each(0, chips - 1, send_pair)

    add_weights()
    add_own()
    each(0, chips - 1, add_pixels)

    for_vars(lambda slot, other: var_copy(slot, other).wait_send())
    each(0, chips - 1, lambda slot: pix_copy(slot).wait_send())
    each(0, chips, lambda slot: sib_copy(slot).wait_send())

    @pl.when(has_l)
    def _():
        edge_copy(0, z - 1).wait_send()

    @pl.when(has_r)
    def _():
        edge_copy(1, z + 1).wait_send()


def per_device(image, variance, mask_bits, boxes, row_filters, col_filters, coeffs):
    height, cols = image.shape[1], image.shape[2]
    visits, skies = lax.axis_size("visit"), lax.axis_size("sky")
    basis = row_filters.shape[0]
    chips = visits // CORES
    few = chips == 4
    deep = basis * WIN
    unit = 16 * PACK
    tall = (height + 2 * LEAD + unit - 1) // unit * unit
    coeffs = jnp.transpose(coeffs, (2, 0, 1))
    hbm = pl.BlockSpec(memory_space=pltpu.HBM)
    f32, bf16 = jnp.float32, jnp.bfloat16
    dma = pltpu.SemaphoreType.DMA
    sums = pl.pallas_call(
        functools.partial(kernel, visits, skies),
        out_shape=jax.ShapeDtypeStruct((2, ROWS_DEV, cols), f32),
        in_specs=[hbm] * 7,
        out_specs=pl.BlockSpec(memory_space=pltpu.VMEM),
        scratch_shapes=[
            pltpu.VMEM((tall + 16, cols), bf16),
            pltpu.VMEM(variance.shape, bf16),
            pltpu.VMEM(mask_bits.shape, jnp.int32),
            pltpu.SMEM(boxes.shape, jnp.int32),
            pltpu.VMEM(row_filters.shape, bf16),
            pltpu.VMEM(col_filters.shape, bf16),
            pltpu.VMEM(coeffs.shape, f32),
            pltpu.VMEM((2, tall // PACK, LANES), bf16),
            pltpu.VMEM((2, tall // PACK, LANES), bf16),
            pltpu.VMEM((tall, cols + LANES), bf16),
            pltpu.VMEM((CORES, chips, ROWS_DEV, cols), bf16),
            pltpu.VMEM((chips, CORES, ROWS_DEV, cols), bf16),
            pltpu.VMEM((chips, ROWS_DEV, cols), f32),
            pltpu.VMEM((chips, ROWS_DEV, cols), f32),
            pltpu.VMEM((chips, ROWS_DEV, cols), f32),
            pltpu.VMEM((chips, ROWS_DEV, cols), bf16),
            pltpu.VMEM((chips, ROWS_DEV, cols), bf16),
            pltpu.VMEM((24, LANES), f32),
            pltpu.VMEM((basis, LANES, 2 * LANES), bf16),
            [pltpu.VMEM((2, tall + 32, cols), bf16)] * (basis // 2),
            pltpu.VMEM((ROWS_DEV, deep), f32),
            pltpu.VMEM((8, deep), f32),
            [pltpu.VMEM((2 * ROWS_DEV, deep), bf16)] * (visits if few else 1),
            pltpu.VMEM((ROWS_DEV, deep), bf16),
            dma((7,)),
            dma((2,)),
            dma((2,)),
            dma((chips, CORES)),
            dma((chips, CORES)),
            dma((chips,)),
            dma((chips,)),
            dma((chips,)),
            dma((chips,)),
        ],
        compiler_params=pltpu.CompilerParams(
            collective_id=0, has_side_effects=True, vmem_limit_bytes=62 * 1024 * 1024
        ),
    )(image, variance, mask_bits, boxes, row_filters, col_filters, coeffs)
    return (sums[0] / jnp.maximum(sums[1], 1.0), sums[1])


def solution(mesh):
    in_specs = (
        P("visit", None, "sky"),
        P("visit", None, "sky"),
        P("visit", None, "sky"),
        P("visit", None),
        P(),
        P(),
        P("visit", None, None),
    )
    out_specs = (P("visit", "sky"), P("visit", "sky"))
    return jax.shard_map(
        per_device, mesh=mesh, in_specs=in_specs, out_specs=out_specs, check_vma=False
    )
```

```python
import functools

import jax
import jax.numpy as jnp
from jax import lax
from jax.experimental import pallas as pl
from jax.experimental.pallas import tpu as pltpu
from jax.sharding import PartitionSpec as P

RAD = 20
ROWS_DEV = 48
REJECT = 7
LANES = 128
CORES = 2
LEAD = 8
TOP = 24
WIN = 2 * ROWS_DEV
UNITS = 2
PACK = 5
TERMS = 6
MESH = pl.DeviceIdType.MESH


def weight_of(plane):
    plane = plane.astype(jnp.float32)
    near = pl.reciprocal(plane, approx=True)
    return jnp.where(plane > 0, near * (2.0 - plane * near), 0.0)


def kernel(
    visits,
    skies,
    image_hbm,
    var_hbm,
    bits_hbm,
    boxes_hbm,
    rowf_hbm,
    colf_hbm,
    coef_hbm,
    sums_ref,
    image_ref,
    var_ref,
    bits_ref,
    boxes_ref,
    rowf_ref,
    colf_ref,
    coef_ref,
    edge_send,
    edge_got,
    wide,
    masked,
    sib_var,
    pair_w,
    got_w,
    own_pix,
    sib_send,
    sib_pix,
    pair_pix,
    got_pix,
    cross_pix,
    got_cross,
    filt,
    col_mats,
    passed,
    toeplitz,
    factors,
    row_mats,
    row_last,
    load_sem,
    halo_send,
    halo_recv,
    var_send,
    var_recv,
    w_send,
    w_recv,
    sib_send_sem,
    sib_recv_sem,
    pix_send,
    pix_recv,
    cross_send,
    cross_recv,
):
    height, cols = var_ref.shape[1], var_ref.shape[2]
    width = cols * skies
    basis, taps = rowf_ref.shape
    blocks = cols // LANES
    inner, outer = units = list(range(1, blocks - 1)), [0, blocks - 1]
    per_unit = blocks // UNITS
    chips = visits // CORES
    few = chips == 4
    deep = basis * WIN
    f32, bf16 = jnp.float32, jnp.bfloat16
    v = lax.axis_index("visit")
    z = lax.axis_index("sky")
    chip = v // CORES
    core = lax.rem(v, CORES)
    sibling = chip * CORES + 1 - core
    has_l = z > 0
    has_r = z < skies - 1

    def chip_at(slot):
        if not few:
            return lax.rem(chip + slot + 1, chips)
        return [chips - 1 - chip, lax.rem(chip + 2, chips), chip + 1 - 2 * lax.rem(chip, 2), chip][slot]

    def each(first, last, body):
        if few:
            for slot in range(first, last):
                body(slot)
        else:

            def one(slot, carry):
                body(slot)
                return carry

            lax.fori_loop(first, last, one, 0)

    barrier = pltpu.get_barrier_semaphore()
    for step in range(1, visits):
        pl.semaphore_signal(
            barrier, inc=1, device_id=(lax.rem(v + step, visits), z), device_id_type=MESH
        )

    @pl.when(has_l)
    def _():
        pl.semaphore_signal(barrier, inc=1, device_id=(v, z - 1), device_id_type=MESH)

    @pl.when(has_r)
    def _():
        pl.semaphore_signal(barrier, inc=1, device_id=(v, z + 1), device_id_type=MESH)

    pairs = (
        (rowf_hbm, rowf_ref),
        (colf_hbm, colf_ref),
        (coef_hbm, coef_ref),
        (image_hbm.at[0], image_ref.at[pl.ds(16, height)]),
        (boxes_hbm, boxes_ref),
        (var_hbm, var_ref),
        (bits_hbm, bits_ref),
    )
    loads = [
        pltpu.make_async_copy(src, dst, load_sem.at[n]) for n, (src, dst) in enumerate(pairs)
    ]
    for load in loads:
        load.start()

    below = image_ref.shape[0] - 16 - height
    image_ref[0:16, :] = jnp.zeros((16, cols), bf16)
    image_ref[16 + height :, :] = jnp.zeros((below, cols), bf16)
    col_first = z * cols
    for pair in passed:
        for h in range(2):
            pair[h, 0:16, :] = jnp.zeros((16, cols), bf16)
            pair[h, pair.shape[1] - 16 :, :] = jnp.zeros((16, cols), bf16)

    for load in loads[:3]:
        load.wait()
    filt[...] = jnp.zeros_like(filt)
    filt[0:basis, 0:taps] = colf_ref[...].astype(f32)
    lane = lax.broadcasted_iota(jnp.int32, (1, LANES), 1)
    ahead = lax.broadcasted_iota(jnp.int32, (LANES, LANES), 1) >= lax.broadcasted_iota(
        jnp.int32, (LANES, LANES), 0
    )

    def build(b):
        col = jnp.broadcast_to(filt[pl.ds(b, 1), :], (LANES, LANES))
        col = pltpu.roll(col, 0, 1, stride=1, stride_axis=0)
        col_mats[b, :, 0:LANES] = jnp.where(ahead, col, 0.0).astype(bf16)
        col_mats[b, :, LANES : 2 * LANES] = jnp.where(ahead, 0.0, col).astype(bf16)

    group_of = lax.broadcasted_iota(jnp.int32, (1, deep), 1) // WIN
    tap_of = lax.broadcasted_iota(jnp.int32, (1, deep), 1) - group_of * WIN - (TOP - RAD)
    tap_mat = (lax.broadcasted_iota(jnp.int32, (taps, deep), 0) == tap_of).astype(f32).astype(bf16)
    own_group = (lax.broadcasted_iota(jnp.int32, (basis, deep), 0) == group_of).astype(f32)
    every = jnp.dot(rowf_ref[...], tap_mat, preferred_element_type=f32)
    line = jnp.sum(every * own_group, axis=0, keepdims=True)
    toeplitz[...] = pltpu.roll(
        jnp.broadcast_to(line, (ROWS_DEV, deep)), 0, 1, stride=1, stride_axis=0
    )
    c = jnp.dot(
        coef_ref[:, 0, :], own_group, precision=lax.Precision.HIGHEST, preferred_element_type=f32
    )
    c = [c[t : t + 1] for t in range(TERMS)]
    xc = (2 * col_first + cols).astype(f32) / width - 1.0
    factors[0:1] = c[0] + xc * (c[1] + xc * c[3])
    factors[1:2] = c[2] + xc * c[4]
    factors[2:3] = c[5]
    factors[3:4] = c[1] + (2.0 * xc) * c[3]
    factors[4:5] = c[4]
    row_last[...] = (toeplitz[...] * c[3]).astype(bf16)
    y_iota = lax.broadcasted_iota(jnp.int32, (ROWS_DEV, LANES), 0)
    tiles = deep // LANES

    def build_rows(band, at, first, last, tie):
        y = (2.0 * (band * ROWS_DEV + y_iota).astype(f32) + 1.0) / height - 1.0 + tie
        for n in range(first, last):
            lanes = slice(n * LANES, (n + 1) * LANES)
            base = toeplitz[:, lanes]
            f = [factors[t : t + 1, lanes] for t in range(5)]
            row_mats[at][0:ROWS_DEV, lanes] = (base * (f[0] + y * (f[1] + y * f[2]))).astype(bf16)
            row_mats[at][ROWS_DEV : 2 * ROWS_DEV, lanes] = (base * (f[3] + y * f[4])).astype(bf16)

    strip = wide.shape[0] // PACK
    loads[3].wait()
    to_l = to_r = jnp.zeros((strip, LANES), f32)
    for g in range(PACK):
        rows = slice(g * strip, (g + 1) * strip)
        part = image_ref[g * strip : (g + 1) * strip + 16, :].astype(f32)[LEAD : LEAD + strip]
        part = pltpu.roll(part, RAD, 1)
        wide[rows, LANES:cols] = part[:, LANES:].astype(bf16)
        edge = part[:, :LANES]
        wide[rows, cols:] = edge.astype(bf16)
        at = g * RAD
        edge = pltpu.roll(edge, at, 1) if g else edge
        to_r = jnp.where((lane >= at) & (lane < at + RAD), edge, to_r)
        to_l = jnp.where((lane >= at + RAD) & (lane < at + 2 * RAD), edge, to_l)
    edge_send[0] = to_l.astype(bf16)
    edge_send[1] = to_r.astype(bf16)

    def remote(src, dst, send, recv, target):
        return pltpu.make_async_remote_copy(
            src_ref=src,
            dst_ref=dst,
            send_sem=send,
            recv_sem=recv,
            device_id=target,
            device_id_type=MESH,
        )

    def edge_copy(side, target):
        return remote(
            edge_send.at[side],
            edge_got.at[side],
            halo_send.at[side],
            halo_recv.at[side],
            (v, target),
        )

    def peer(slot):
        return (chip_at(slot) * CORES + core, z)

    def var_copy():
        return remote(masked.at[1 - core], sib_var, var_send.at[0], var_recv.at[0], (sibling, z))

    def w_copy(slot):
        return remote(
            pair_w.at[slot], got_w.at[slot], w_send.at[slot], w_recv.at[slot], peer(slot)
        )

    def sib_copy(unit, slot):
        return remote(
            sib_send.at[unit, slot],
            sib_pix.at[unit, slot],
            sib_send_sem.at[unit, slot],
            sib_recv_sem.at[unit, slot],
            (sibling, z),
        )

    def pix_copy(unit, slot):
        return remote(
            pair_pix.at[unit, slot],
            got_pix.at[unit, slot],
            pix_send.at[unit, slot],
            pix_recv.at[unit, slot],
            peer(slot),
        )

    def cross_copy():
        target = (chip_at(2) * CORES + 1 - core, z)
        return remote(cross_pix, got_cross, cross_send.at[0], cross_recv.at[0], target)

    pl.semaphore_wait(barrier, visits - 1 + has_l.astype(jnp.int32) + has_r.astype(jnp.int32))

    @pl.when(has_l)
    def _():
        edge_copy(0, z - 1).start()

    @pl.when(has_r)
    def _():
        edge_copy(1, z + 1).start()

    for load in loads[4:]:
        load.wait()
    box = [boxes_ref[0, i] for i in range(4)]
    col_index = col_first + lax.broadcasted_iota(jnp.int32, (ROWS_DEV, cols), 1)
    col_inside = (col_index >= box[2]) & (col_index < box[3])
    row_iota = lax.broadcasted_iota(jnp.int32, (ROWS_DEV, cols), 0)

    def mask_band(band, carry):
        first = pl.multiple_of(band * ROWS_DEV, ROWS_DEV)
        rows = pl.ds(first, ROWS_DEV)
        row_index = first + row_iota
        inside = (row_index >= box[0]) & (row_index < box[1]) & col_inside
        inside = inside & ((bits_ref[0, rows, :] & REJECT) == 0)
        masked[lax.rem(band, CORES), band // CORES] = jnp.where(
            inside, var_ref[0, rows, :].astype(f32), 0.0
        ).astype(bf16)
        return carry

    lax.fori_loop(0, visits, mask_band, 0, unroll=few)
    var_copy().start()

    def col_step(p, first, rows, which):
        parts = [wide[pl.ds(first, rows), k * LANES : (k + 2) * LANES] for k in which]
        mats = col_mats[pl.ds(2 * p, 2)].reshape(2 * LANES, 2 * LANES)
        out = lax.dot_general(
            jnp.concatenate(parts, axis=0),
            mats,
            (((1,), (1,)), ((), ())),
            preferred_element_type=f32,
        )
        into = pl.ds(pl.multiple_of(first + 16, 16), rows)
        for n, k in enumerate(which):
            for h in range(2):
                passed[p][h, into, k * LANES : (k + 1) * LANES] = out[
                    n * rows : (n + 1) * rows, h * LANES : (h + 1) * LANES
                ].astype(bf16)
        return out[0:1, 0:LANES] * 0.0

    def weighted(unit, slot, side, at):
        which = units[unit]
        at_chip = chip_at(slot)
        band = at_chip * CORES + side
        if not few:
            build_rows(band, at, 0, tiles, 0.0)
        rows = pl.ds(pl.multiple_of(band * ROWS_DEV, 16), WIN)
        mats = jnp.concatenate([row_mats[at][...], row_last[...]], axis=0)
        lines = jnp.concatenate(
            [
                jnp.concatenate(
                    [
                        pair[:, rows, k * LANES : (k + 1) * LANES].reshape(2 * WIN, LANES)
                        for pair in passed
                    ],
                    axis=0,
                )
                for k in which
            ],
            axis=1,
        )
        out = jnp.dot(mats, lines, preferred_element_type=f32)
        x = jnp.concatenate(
            [(2 * (k * LANES + lane) + 1 - cols).astype(f32) / width for k in which], axis=1
        )
        pixels = out[0:ROWS_DEV] + x * (
            out[ROWS_DEV : 2 * ROWS_DEV] + x * out[2 * ROWS_DEV : 3 * ROWS_DEV]
        )
        plane = masked[side, at_chip]
        plane = jnp.concatenate([plane[:, k * LANES : (k + 1) * LANES] for k in which], axis=1)
        return pixels * weight_of(plane), out[0:1, 0:LANES] * 0.0

    def for_sibling(unit, slot, at=0):
        sib_send[unit, slot], tie = weighted(unit, slot, 1 - core, at)
        return tie

    def for_own(unit, slot, at=0):
        own_pix[unit, slot], tie = weighted(unit, slot, core, at)
        return tie

    def send_pair(unit, slot):
        sib_copy(unit, slot).wait_recv()
        pair_pix[unit, slot] = (own_pix[unit, slot] + sib_pix[unit, slot]).astype(bf16)
        pix_copy(unit, slot).start()

    def pair_weight(slot):
        at_chip = chip_at(slot)
        return weight_of(masked[core, at_chip]) + weight_of(sib_var[at_chip])

    def send_weight(slot):
        pair_w[slot] = pair_weight(slot).astype(bf16)
        w_copy(slot).start()

    def edges():
        @pl.when(has_l)
        def _():
            edge_copy(1, z - 1).wait_recv()

        @pl.when(has_r)
        def _():
            edge_copy(0, z + 1).wait_recv()

        @pl.when(jnp.logical_not(has_l))
        def _():
            edge_got[1] = jnp.zeros((strip, LANES), bf16)

        @pl.when(jnp.logical_not(has_r))
        def _():
            edge_got[0] = jnp.zeros((strip, LANES), bf16)

    def merge_edges():
        for g in range(PACK):
            rows = slice(g * strip, (g + 1) * strip)
            mine = wide[rows, cols:].astype(f32)
            from_r, from_l = (edge_got[side].astype(f32) for side in range(2))
            if g:
                from_r = pltpu.roll(from_r, LANES - g * RAD, 1)
                from_l = pltpu.roll(from_l, LANES - g * RAD, 1)
            wide[rows, 0:LANES] = jnp.where(lane < RAD, from_l, mine).astype(bf16)
            wide[rows, cols:] = jnp.where(
                (lane >= RAD) & (lane < 2 * RAD), from_r, mine
            ).astype(bf16)

    def add_weights():
        sums_ref[1] = pair_weight(chips - 1)

        def one(slot):
            w_copy(slot).wait_recv()
            sums_ref[1] += got_w[slot].astype(f32)

        each(0, chips - 1, one)

    def in_place(plane_of):
        lanes_of = {}
        for unit, which in enumerate(units):
            part = plane_of(unit)
            for n, k in enumerate(which):
                lanes_of[k] = part[:, n * LANES : (n + 1) * LANES]
        return jnp.concatenate([lanes_of[k] for k in range(blocks)], axis=1)

    def add_to(unit, value, first=False):
        for n, k in enumerate(units[unit]):
            lanes = slice(k * LANES, (k + 1) * LANES)
            part = value[:, n * LANES : (n + 1) * LANES]
            sums_ref[0, :, lanes] = part if first else sums_ref[0, :, lanes] + part

    def add_own(unit):
        sib_copy(unit, chips - 1).wait_recv()
        add_to(unit, own_pix[unit, chips - 1] + sib_pix[unit, chips - 1], True)

    def add_pixels(unit, slot):
        pix_copy(unit, slot).wait_recv()
        add_to(unit, got_pix[unit, slot].astype(f32))

    steps = basis // 2
    if few:
        half = chips // 2 * CORES * ROWS_DEV
        group = chip // 2
        total = height + 2 * LEAD
        early = half + 2 * LEAD + LEAD * 2
        far = pl.multiple_of((1 - group) * (total - early), 16)
        near = pl.multiple_of(group * early, 16)
        bands = [(0, 1), (1, 1), (2, 1), (0, 0), (1, 0), (2, 0), (3, 1), (3, 0)]

        def band_of(at):
            slot, other = bands[at]
            return chip_at(slot) * CORES + (1 - core if other else core)

        def columns(first, rows, which, base, count, build_too=False):
            pieces = [(base + n // tiles, n % tiles) for n in range(count * tiles)]
            each_step = -(-len(pieces) // steps)
            for p in range(steps):
                if build_too:
                    build(2 * p)
                    build(2 * p + 1)
                tie = col_step(p, first, rows, which)
                mine = pieces[p * each_step : (p + 1) * each_step]
                for at in sorted({at for at, _ in mine}):
                    of = [n for a, n in mine if a == at]
                    build_rows(band_of(at), at, of[0], of[-1] + 1, tie)

        def rows_beside(at, tie):
            build_rows(band_of(at), at, 0, tiles, tie)

        columns(far, early, inner, 0, 2, True)
        columns(near, total - early, inner, 2, 3)
        rows_beside(5, for_sibling(0, 0, 0))
        for_sibling(0, 1, 1)
        for_sibling(0, 2, 2)
        for_own(0, 0, 3)
        var_copy().wait_recv()
        for slot in range(3):
            send_weight(slot)
            sib_copy(0, slot).start()
        tie = for_own(0, 1, 4)
        rows_beside(6, tie)
        rows_beside(7, tie)
        for_own(0, 2, 5)
        for_sibling(0, 3, 6)
        for_own(0, 3, 7)
        edges()
        sib_copy(0, 3).start()
        merge_edges()
        columns(far, early, outer, 0, 0)
        for slot in range(2):
            for_sibling(1, slot, slot)
        for slot in range(2):
            sib_copy(1, slot).start()
        for slot in range(3):
            send_pair(0, slot)
        for slot in range(2):
            for_own(1, slot, 3 + slot)
        columns(near, total - early, outer, 0, 0)
        cross_pix[...] = weighted(1, 2, 1 - core, 2)[0].astype(bf16)
        pair_pix[1, 2] = weighted(1, 2, core, 5)[0].astype(bf16)
        for slot in range(2):
            send_pair(1, slot)
        cross_copy().start()
        pix_copy(1, 2).start()
        for_sibling(1, 3, 6)
        for_own(1, 3, 7)
        sib_copy(1, 3).start()
    else:
        edges()
        merge_edges()
        for b in range(basis):
            build(b)

        def one(g, carry):
            for p in range(steps):
                for which in units:
                    col_step(p, pl.multiple_of(g * strip, 16), strip, which)
            return carry

        lax.fori_loop(0, PACK, one, 0)
        var_copy().wait_recv()
        each(0, chips - 1, send_weight)
        for unit in range(UNITS):

            def sibling_band(slot):
                for_sibling(unit, slot)
                sib_copy(unit, slot).start()

            each(0, chips, sibling_band)
            each(0, chips, lambda slot: for_own(unit, slot))
            each(0, chips - 1, lambda slot: send_pair(unit, slot))

    add_weights()
    add_own(0)
    each(0, chips - 1, lambda slot: add_pixels(0, slot))
    add_own(1)

    var_copy().wait_send()

    def drain(slot):
        w_copy(slot).wait_send()
        for unit in range(UNITS):
            pix_copy(unit, slot).wait_send()

    each(0, chips - 1, drain)
    for unit in range(UNITS):
        each(
            0,
            chips,
            lambda slot: None if few and (unit, slot) == (1, 2) else sib_copy(unit, slot).wait_send(),
        )

    @pl.when(has_l)
    def _():
        edge_copy(0, z - 1).wait_send()

    @pl.when(has_r)
    def _():
        edge_copy(1, z + 1).wait_send()

    if few:
        cross_copy().wait_send()
        add_pixels(1, 2)
        cross_copy().wait_recv()
        add_to(1, got_cross[...].astype(f32))
        add_pixels(1, 1)
        add_pixels(1, 0)
    else:
        each(0, chips - 1, lambda slot: add_pixels(1, slot))


def per_device(image, variance, mask_bits, boxes, row_filters, col_filters, coeffs):
    height, cols = image.shape[1], image.shape[2]
    visits, skies = lax.axis_size("visit"), lax.axis_size("sky")
    basis = row_filters.shape[0]
    chips = visits // CORES
    few = chips == 4
    deep = basis * WIN
    span = cols // UNITS
    unit = 16 * PACK
    tall = (height + 2 * LEAD + unit - 1) // unit * unit
    coeffs = jnp.transpose(coeffs, (2, 0, 1))
    hbm = pl.BlockSpec(memory_space=pltpu.HBM)
    f32, bf16 = jnp.float32, jnp.bfloat16
    dma = pltpu.SemaphoreType.DMA
    sums = pl.pallas_call(
        functools.partial(kernel, visits, skies),
        out_shape=jax.ShapeDtypeStruct((2, ROWS_DEV, cols), f32),
        in_specs=[hbm] * 7,
        out_specs=pl.BlockSpec(memory_space=pltpu.VMEM),
        scratch_shapes=[
            pltpu.VMEM((tall + 16, cols), bf16),
            pltpu.VMEM(variance.shape, bf16),
            pltpu.VMEM(mask_bits.shape, jnp.int32),
            pltpu.SMEM(boxes.shape, jnp.int32),
            pltpu.VMEM(row_filters.shape, bf16),
            pltpu.VMEM(col_filters.shape, bf16),
            pltpu.VMEM(coeffs.shape, f32),
            pltpu.VMEM((2, tall // PACK, LANES), bf16),
            pltpu.VMEM((2, tall // PACK, LANES), bf16),
            pltpu.VMEM((tall, cols + LANES), bf16),
            pltpu.VMEM((CORES, chips, ROWS_DEV, cols), bf16),
            pltpu.VMEM((chips, ROWS_DEV, cols), bf16),
            pltpu.VMEM((chips, ROWS_DEV, cols), bf16),
            pltpu.VMEM((chips, ROWS_DEV, cols), bf16),
            pltpu.VMEM((UNITS, chips, ROWS_DEV, span), f32),
            pltpu.VMEM((UNITS, chips, ROWS_DEV, span), f32),
            pltpu.VMEM((UNITS, chips, ROWS_DEV, span), f32),
            pltpu.VMEM((UNITS, chips, ROWS_DEV, span), bf16),
            pltpu.VMEM((UNITS, chips, ROWS_DEV, span), bf16),
            pltpu.VMEM((ROWS_DEV, span), bf16),
            pltpu.VMEM((ROWS_DEV, span), bf16),
            pltpu.VMEM((24, LANES), f32),
            pltpu.VMEM((basis, LANES, 2 * LANES), bf16),
            [pltpu.VMEM((2, tall + 32, cols), bf16)] * (basis // 2),
            pltpu.VMEM((ROWS_DEV, deep), f32),
            pltpu.VMEM((8, deep), f32),
            [pltpu.VMEM((2 * ROWS_DEV, deep), bf16)] * (visits if few else 1),
            pltpu.VMEM((ROWS_DEV, deep), bf16),
            dma((7,)),
            dma((2,)),
            dma((2,)),
            dma((1,)),
            dma((1,)),
            dma((chips,)),
            dma((chips,)),
            dma((UNITS, chips)),
            dma((UNITS, chips)),
            dma((UNITS, chips)),
            dma((UNITS, chips)),
            dma((1,)),
            dma((1,)),
        ],
        compiler_params=pltpu.CompilerParams(
            collective_id=0, has_side_effects=True, vmem_limit_bytes=62 * 1024 * 1024
        ),
    )(image, variance, mask_bits, boxes, row_filters, col_filters, coeffs)
    return (sums[0] / jnp.maximum(sums[1], 1.0), sums[1])


def solution(mesh):
    in_specs = (
        P("visit", None, "sky"),
        P("visit", None, "sky"),
        P("visit", None, "sky"),
        P("visit", None),
        P(),
        P(),
        P("visit", None, None),
    )
    out_specs = (P("visit", "sky"), P("visit", "sky"))
    return jax.shard_map(
        per_device, mesh=mesh, in_specs=in_specs, out_specs=out_specs, check_vma=False
    )
```

```python
import functools

import jax
import jax.numpy as jnp
from jax import lax
from jax.experimental import pallas as pl
from jax.experimental.pallas import tpu as pltpu
from jax.sharding import PartitionSpec as P

RAD = 20
ROWS_DEV = 48
REJECT = 7
LANES = 128
CORES = 2
LEAD = 8
TOP = 24
WIN = 2 * ROWS_DEV
UNITS = 2
PACK = 5
TERMS = 6
MESH = pl.DeviceIdType.MESH


def weight_of(plane):
    plane = plane.astype(jnp.float32)
    near = pl.reciprocal(plane, approx=True)
    return jnp.where(plane > 0, near * (2.0 - plane * near), 0.0)


def kernel(
    visits,
    skies,
    image_hbm,
    var_hbm,
    bits_hbm,
    boxes_hbm,
    rowf_hbm,
    colf_hbm,
    coef_hbm,
    sums_ref,
    image_ref,
    var_ref,
    bits_ref,
    boxes_ref,
    rowf_ref,
    colf_ref,
    coef_ref,
    edge_send,
    edge_got,
    wide,
    masked,
    got_var,
    own_pix,
    sib_send,
    sib_pix,
    pair_pix,
    got_pix,
    cross_pix,
    got_cross,
    filt,
    col_mats,
    passed,
    toeplitz,
    factors,
    row_mats,
    row_last,
    load_sem,
    halo_send,
    halo_recv,
    var_send,
    var_recv,
    sib_send_sem,
    sib_recv_sem,
    pix_send,
    pix_recv,
    cross_send,
    cross_recv,
):
    height, cols = var_ref.shape[1], var_ref.shape[2]
    width = cols * skies
    basis, taps = rowf_ref.shape
    blocks = cols // LANES
    inner, outer = units = list(range(1, blocks - 1)), [0, blocks - 1]
    per_unit = blocks // UNITS
    chips = visits // CORES
    few = chips == 4
    deep = basis * WIN
    f32, bf16 = jnp.float32, jnp.bfloat16
    v = lax.axis_index("visit")
    z = lax.axis_index("sky")
    chip = v // CORES
    core = lax.rem(v, CORES)
    sibling = chip * CORES + 1 - core
    has_l = z > 0
    has_r = z < skies - 1

    def chip_at(slot):
        if not few:
            return lax.rem(chip + slot + 1, chips)
        return [chips - 1 - chip, lax.rem(chip + 2, chips), chip + 1 - 2 * lax.rem(chip, 2), chip][slot]

    def each(first, last, body):
        if few:
            for slot in range(first, last):
                body(slot)
        else:

            def one(slot, carry):
                body(slot)
                return carry

            lax.fori_loop(first, last, one, 0)

    barrier = pltpu.get_barrier_semaphore()
    for step in range(1, visits):
        pl.semaphore_signal(
            barrier, inc=1, device_id=(lax.rem(v + step, visits), z), device_id_type=MESH
        )

    @pl.when(has_l)
    def _():
        pl.semaphore_signal(barrier, inc=1, device_id=(v, z - 1), device_id_type=MESH)

    @pl.when(has_r)
    def _():
        pl.semaphore_signal(barrier, inc=1, device_id=(v, z + 1), device_id_type=MESH)

    pairs = (
        (rowf_hbm, rowf_ref),
        (colf_hbm, colf_ref),
        (coef_hbm, coef_ref),
        (image_hbm.at[0], image_ref.at[pl.ds(16, height)]),
        (boxes_hbm, boxes_ref),
        (var_hbm, var_ref),
        (bits_hbm, bits_ref),
    )
    loads = [
        pltpu.make_async_copy(src, dst, load_sem.at[n]) for n, (src, dst) in enumerate(pairs)
    ]
    for load in loads:
        load.start()

    below = image_ref.shape[0] - 16 - height
    image_ref[0:16, :] = jnp.zeros((16, cols), bf16)
    image_ref[16 + height :, :] = jnp.zeros((below, cols), bf16)
    col_first = z * cols
    for pair in passed:
        for h in range(2):
            pair[h, 0:16, :] = jnp.zeros((16, cols), bf16)
            pair[h, pair.shape[1] - 16 :, :] = jnp.zeros((16, cols), bf16)

    for load in loads[:3]:
        load.wait()
    filt[...] = jnp.zeros_like(filt)
    filt[0:basis, 0:taps] = colf_ref[...].astype(f32)
    lane = lax.broadcasted_iota(jnp.int32, (1, LANES), 1)
    ahead = lax.broadcasted_iota(jnp.int32, (LANES, LANES), 1) >= lax.broadcasted_iota(
        jnp.int32, (LANES, LANES), 0
    )

    def build(b):
        col = jnp.broadcast_to(filt[pl.ds(b, 1), :], (LANES, LANES))
        col = pltpu.roll(col, 0, 1, stride=1, stride_axis=0)
        col_mats[b, :, 0:LANES] = jnp.where(ahead, col, 0.0).astype(bf16)
        col_mats[b, :, LANES : 2 * LANES] = jnp.where(ahead, 0.0, col).astype(bf16)

    group_of = lax.broadcasted_iota(jnp.int32, (1, deep), 1) // WIN
    tap_of = lax.broadcasted_iota(jnp.int32, (1, deep), 1) - group_of * WIN - (TOP - RAD)
    tap_mat = (lax.broadcasted_iota(jnp.int32, (taps, deep), 0) == tap_of).astype(f32).astype(bf16)
    own_group = (lax.broadcasted_iota(jnp.int32, (basis, deep), 0) == group_of).astype(f32)
    every = jnp.dot(rowf_ref[...], tap_mat, preferred_element_type=f32)
    line = jnp.sum(every * own_group, axis=0, keepdims=True)
    toeplitz[...] = pltpu.roll(
        jnp.broadcast_to(line, (ROWS_DEV, deep)), 0, 1, stride=1, stride_axis=0
    )
    c = jnp.dot(
        coef_ref[:, 0, :], own_group, precision=lax.Precision.HIGHEST, preferred_element_type=f32
    )
    c = [c[t : t + 1] for t in range(TERMS)]
    xc = (2 * col_first + cols).astype(f32) / width - 1.0
    factors[0:1] = c[0] + xc * (c[1] + xc * c[3])
    factors[1:2] = c[2] + xc * c[4]
    factors[2:3] = c[5]
    factors[3:4] = c[1] + (2.0 * xc) * c[3]
    factors[4:5] = c[4]
    row_last[...] = (toeplitz[...] * c[3]).astype(bf16)
    y_iota = lax.broadcasted_iota(jnp.int32, (ROWS_DEV, LANES), 0)
    tiles = deep // LANES

    def build_rows(band, at, first, last, tie):
        y = (2.0 * (band * ROWS_DEV + y_iota).astype(f32) + 1.0) / height - 1.0 + tie
        for n in range(first, last):
            lanes = slice(n * LANES, (n + 1) * LANES)
            base = toeplitz[:, lanes]
            f = [factors[t : t + 1, lanes] for t in range(5)]
            row_mats[at][0:ROWS_DEV, lanes] = (base * (f[0] + y * (f[1] + y * f[2]))).astype(bf16)
            row_mats[at][ROWS_DEV : 2 * ROWS_DEV, lanes] = (base * (f[3] + y * f[4])).astype(bf16)

    strip = wide.shape[0] // PACK
    loads[3].wait()
    to_l = to_r = jnp.zeros((strip, LANES), f32)
    for g in range(PACK):
        rows = slice(g * strip, (g + 1) * strip)
        part = image_ref[g * strip : (g + 1) * strip + 16, :].astype(f32)[LEAD : LEAD + strip]
        part = pltpu.roll(part, RAD, 1)
        wide[rows, LANES:cols] = part[:, LANES:].astype(bf16)
        edge = part[:, :LANES]
        wide[rows, cols:] = edge.astype(bf16)
        at = g * RAD
        edge = pltpu.roll(edge, at, 1) if g else edge
        to_r = jnp.where((lane >= at) & (lane < at + RAD), edge, to_r)
        to_l = jnp.where((lane >= at + RAD) & (lane < at + 2 * RAD), edge, to_l)
    edge_send[0] = to_l.astype(bf16)
    edge_send[1] = to_r.astype(bf16)

    def remote(src, dst, send, recv, target):
        return pltpu.make_async_remote_copy(
            src_ref=src,
            dst_ref=dst,
            send_sem=send,
            recv_sem=recv,
            device_id=target,
            device_id_type=MESH,
        )

    def edge_copy(side, target):
        return remote(
            edge_send.at[side],
            edge_got.at[side],
            halo_send.at[side],
            halo_recv.at[side],
            (v, target),
        )

    def peer(slot):
        return (chip_at(slot) * CORES + core, z)

    def var_copy(slot, other):
        side = 1 - core if other else core
        return remote(
            masked.at[side, chip_at(slot)],
            got_var.at[slot, other],
            var_send.at[slot, other],
            var_recv.at[slot, other],
            (chip_at(slot) * CORES + side, z),
        )

    def for_vars(act):
        def both(slot):
            act(slot, 0)
            act(slot, 1)

        each(0, chips - 1, both)
        act(chips - 1, 1)

    def sib_copy(unit, slot):
        return remote(
            sib_send.at[unit, slot],
            sib_pix.at[unit, slot],
            sib_send_sem.at[unit, slot],
            sib_recv_sem.at[unit, slot],
            (sibling, z),
        )

    def pix_copy(unit, slot):
        return remote(
            pair_pix.at[unit, slot],
            got_pix.at[unit, slot],
            pix_send.at[unit, slot],
            pix_recv.at[unit, slot],
            peer(slot),
        )

    def cross_copy():
        target = (chip_at(2) * CORES + 1 - core, z)
        return remote(cross_pix, got_cross, cross_send.at[0], cross_recv.at[0], target)

    pl.semaphore_wait(barrier, visits - 1 + has_l.astype(jnp.int32) + has_r.astype(jnp.int32))

    @pl.when(has_l)
    def _():
        edge_copy(0, z - 1).start()

    @pl.when(has_r)
    def _():
        edge_copy(1, z + 1).start()

    for load in loads[4:]:
        load.wait()
    box = [boxes_ref[0, i] for i in range(4)]
    col_index = col_first + lax.broadcasted_iota(jnp.int32, (1, cols), 1)
    col_out = jnp.where((col_index >= box[2]) & (col_index < box[3]), 0, 1)
    row_iota = lax.broadcasted_iota(jnp.int32, (ROWS_DEV, LANES), 0)

    def mask_band(band, carry):
        first = pl.multiple_of(band * ROWS_DEV, ROWS_DEV)
        rows = pl.ds(first, ROWS_DEV)
        row_index = first + row_iota
        row_out = jnp.where((row_index >= box[0]) & (row_index < box[1]), 0, 1)
        row_out = jnp.concatenate([row_out] * blocks, axis=1)
        out = (bits_ref[0, rows, :] & REJECT) | row_out | col_out
        masked[lax.rem(band, CORES), band // CORES] = jnp.where(
            out == 0, var_ref[0, rows, :].astype(f32), 0.0
        ).astype(bf16)
        return carry

    lax.fori_loop(0, visits, mask_band, 0, unroll=few)
    for_vars(lambda slot, other: var_copy(slot, other).start())

    def col_step(p, first, rows, which):
        parts = [wide[pl.ds(first, rows), k * LANES : (k + 2) * LANES] for k in which]
        mats = col_mats[pl.ds(2 * p, 2)].reshape(2 * LANES, 2 * LANES)
        out = lax.dot_general(
            jnp.concatenate(parts, axis=0),
            mats,
            (((1,), (1,)), ((), ())),
            preferred_element_type=f32,
        )
        into = pl.ds(pl.multiple_of(first + 16, 16), rows)
        for n, k in enumerate(which):
            for h in range(2):
                passed[p][h, into, k * LANES : (k + 1) * LANES] = out[
                    n * rows : (n + 1) * rows, h * LANES : (h + 1) * LANES
                ].astype(bf16)
        return out[0:1, 0:LANES] * 0.0

    def weighted(unit, slot, side, at):
        which = units[unit]
        at_chip = chip_at(slot)
        band = at_chip * CORES + side
        if not few:
            build_rows(band, at, 0, tiles, 0.0)
        rows = pl.ds(pl.multiple_of(band * ROWS_DEV, 16), WIN)
        mats = jnp.concatenate([row_mats[at][...], row_last[...]], axis=0)
        lines = jnp.concatenate(
            [
                jnp.concatenate(
                    [
                        pair[:, rows, k * LANES : (k + 1) * LANES].reshape(2 * WIN, LANES)
                        for pair in passed
                    ],
                    axis=0,
                )
                for k in which
            ],
            axis=1,
        )
        out = jnp.dot(mats, lines, preferred_element_type=f32)
        x = jnp.concatenate(
            [(2 * (k * LANES + lane) + 1 - cols).astype(f32) / width for k in which], axis=1
        )
        pixels = out[0:ROWS_DEV] + x * (
            out[ROWS_DEV : 2 * ROWS_DEV] + x * out[2 * ROWS_DEV : 3 * ROWS_DEV]
        )
        plane = masked[side, at_chip]
        plane = jnp.concatenate([plane[:, k * LANES : (k + 1) * LANES] for k in which], axis=1)
        return pixels * weight_of(plane), out[0:1, 0:LANES] * 0.0

    def for_sibling(unit, slot, at=0):
        sib_send[unit, slot], tie = weighted(unit, slot, 1 - core, at)
        return tie

    def for_own(unit, slot, at=0):
        own_pix[unit, slot], tie = weighted(unit, slot, core, at)
        return tie

    def send_pair(unit, slot):
        sib_copy(unit, slot).wait_recv()
        pair_pix[unit, slot] = (own_pix[unit, slot] + sib_pix[unit, slot]).astype(bf16)
        pix_copy(unit, slot).start()

    def edges():
        @pl.when(has_l)
        def _():
            edge_copy(1, z - 1).wait_recv()

        @pl.when(has_r)
        def _():
            edge_copy(0, z + 1).wait_recv()

        @pl.when(jnp.logical_not(has_l))
        def _():
            edge_got[1] = jnp.zeros((strip, LANES), bf16)

        @pl.when(jnp.logical_not(has_r))
        def _():
            edge_got[0] = jnp.zeros((strip, LANES), bf16)

    def merge_edges():
        for g in range(PACK):
            rows = slice(g * strip, (g + 1) * strip)
            mine = wide[rows, cols:].astype(f32)
            from_r, from_l = (edge_got[side].astype(f32) for side in range(2))
            if g:
                from_r = pltpu.roll(from_r, LANES - g * RAD, 1)
                from_l = pltpu.roll(from_l, LANES - g * RAD, 1)
            wide[rows, 0:LANES] = jnp.where(lane < RAD, from_l, mine).astype(bf16)
            wide[rows, cols:] = jnp.where(
                (lane >= RAD) & (lane < 2 * RAD), from_r, mine
            ).astype(bf16)

    def add_weights():
        sums_ref[1] = weight_of(masked[core, chip])

        def one(slot, other):
            var_copy(slot, other).wait_recv()
            sums_ref[1] += weight_of(got_var[slot, other])

        for_vars(one)

    def in_place(plane_of):
        lanes_of = {}
        for unit, which in enumerate(units):
            part = plane_of(unit)
            for n, k in enumerate(which):
                lanes_of[k] = part[:, n * LANES : (n + 1) * LANES]
        return jnp.concatenate([lanes_of[k] for k in range(blocks)], axis=1)

    def add_to(unit, value, first=False):
        for n, k in enumerate(units[unit]):
            lanes = slice(k * LANES, (k + 1) * LANES)
            part = value[:, n * LANES : (n + 1) * LANES]
            sums_ref[0, :, lanes] = part if first else sums_ref[0, :, lanes] + part

    def add_own(unit):
        sib_copy(unit, chips - 1).wait_recv()
        add_to(unit, own_pix[unit, chips - 1] + sib_pix[unit, chips - 1], True)

    def add_pixels(unit, slot):
        pix_copy(unit, slot).wait_recv()
        add_to(unit, got_pix[unit, slot].astype(f32))

    steps = basis // 2
    if few:
        half = chips // 2 * CORES * ROWS_DEV
        group = chip // 2
        total = height + 2 * LEAD
        early = half + 2 * LEAD + LEAD * 2
        far = pl.multiple_of((1 - group) * (total - early), 16)
        near = pl.multiple_of(group * early, 16)
        bands = [(0, 1), (1, 1), (2, 1), (0, 0), (1, 0), (2, 0), (3, 1), (3, 0)]

        def band_of(at):
            slot, other = bands[at]
            return chip_at(slot) * CORES + (1 - core if other else core)

        def columns(first, rows, which, base, count, build_too=False):
            pieces = [(base + n // tiles, n % tiles) for n in range(count * tiles)]
            each_step = -(-len(pieces) // steps)
            for p in range(steps):
                if build_too:
                    build(2 * p)
                    build(2 * p + 1)
                tie = col_step(p, first, rows, which)
                mine = pieces[p * each_step : (p + 1) * each_step]
                for at in sorted({at for at, _ in mine}):
                    of = [n for a, n in mine if a == at]
                    build_rows(band_of(at), at, of[0], of[-1] + 1, tie)

        def rows_beside(at, tie):
            build_rows(band_of(at), at, 0, tiles, tie)

        columns(far, early, inner, 0, 2, True)
        columns(near, total - early, inner, 2, 3)
        rows_beside(5, for_sibling(0, 0, 0))
        for_sibling(0, 1, 1)
        for_sibling(0, 2, 2)
        for_own(0, 0, 3)
        tie = for_own(0, 1, 4)
        rows_beside(6, tie)
        rows_beside(7, tie)
        for_own(0, 2, 5)
        edges()
        for slot in range(3):
            sib_copy(0, slot).start()
        merge_edges()
        columns(far, early, outer, 0, 0)
        for slot in range(2):
            for_sibling(1, slot, slot)
        for slot in range(2):
            sib_copy(1, slot).start()
        for slot in range(3):
            send_pair(0, slot)
        for slot in range(2):
            for_own(1, slot, 3 + slot)
        for_sibling(0, 3, 6)
        for_own(0, 3, 7)
        for slot in range(2):
            send_pair(1, slot)
        sib_copy(0, 3).start()
        columns(near, total - early, outer, 0, 0)
        cross_pix[...] = weighted(1, 2, 1 - core, 2)[0].astype(bf16)
        pair_pix[1, 2] = weighted(1, 2, core, 5)[0].astype(bf16)
        cross_copy().start()
        pix_copy(1, 2).start()
        for_sibling(1, 3, 6)
        for_own(1, 3, 7)
        sib_copy(1, 3).start()
    else:
        edges()
        merge_edges()
        for b in range(basis):
            build(b)

        def one(g, carry):
            for p in range(steps):
                for which in units:
                    col_step(p, pl.multiple_of(g * strip, 16), strip, which)
            return carry

        lax.fori_loop(0, PACK, one, 0)
        for unit in range(UNITS):

            def sibling_band(slot):
                for_sibling(unit, slot)
                sib_copy(unit, slot).start()

            each(0, chips, sibling_band)
            each(0, chips, lambda slot: for_own(unit, slot))
            each(0, chips - 1, lambda slot: send_pair(unit, slot))

    add_weights()
    add_own(0)
    each(0, chips - 1, lambda slot: add_pixels(0, slot))
    add_own(1)

    for_vars(lambda slot, other: var_copy(slot, other).wait_send())

    def drain(slot):
        for unit in range(UNITS):
            pix_copy(unit, slot).wait_send()

    each(0, chips - 1, drain)
    for unit in range(UNITS):
        each(
            0,
            chips,
            lambda slot: None if few and (unit, slot) == (1, 2) else sib_copy(unit, slot).wait_send(),
        )

    @pl.when(has_l)
    def _():
        edge_copy(0, z - 1).wait_send()

    @pl.when(has_r)
    def _():
        edge_copy(1, z + 1).wait_send()

    if few:
        cross_copy().wait_send()
        add_pixels(1, 2)
        cross_copy().wait_recv()
        add_to(1, got_cross[...].astype(f32))
        add_pixels(1, 1)
        add_pixels(1, 0)
    else:
        each(0, chips - 1, lambda slot: add_pixels(1, slot))


def per_device(image, variance, mask_bits, boxes, row_filters, col_filters, coeffs):
    height, cols = image.shape[1], image.shape[2]
    visits, skies = lax.axis_size("visit"), lax.axis_size("sky")
    basis = row_filters.shape[0]
    chips = visits // CORES
    few = chips == 4
    deep = basis * WIN
    span = cols // UNITS
    unit = 16 * PACK
    tall = (height + 2 * LEAD + unit - 1) // unit * unit
    coeffs = jnp.transpose(coeffs, (2, 0, 1))
    hbm = pl.BlockSpec(memory_space=pltpu.HBM)
    f32, bf16 = jnp.float32, jnp.bfloat16
    dma = pltpu.SemaphoreType.DMA
    sums = pl.pallas_call(
        functools.partial(kernel, visits, skies),
        out_shape=jax.ShapeDtypeStruct((2, ROWS_DEV, cols), f32),
        in_specs=[hbm] * 7,
        out_specs=pl.BlockSpec(memory_space=pltpu.VMEM),
        scratch_shapes=[
            pltpu.VMEM((tall + 16, cols), bf16),
            pltpu.VMEM(variance.shape, bf16),
            pltpu.VMEM(mask_bits.shape, jnp.int32),
            pltpu.SMEM(boxes.shape, jnp.int32),
            pltpu.VMEM(row_filters.shape, bf16),
            pltpu.VMEM(col_filters.shape, bf16),
            pltpu.VMEM(coeffs.shape, f32),
            pltpu.VMEM((2, tall // PACK, LANES), bf16),
            pltpu.VMEM((2, tall // PACK, LANES), bf16),
            pltpu.VMEM((tall, cols + LANES), bf16),
            pltpu.VMEM((CORES, chips, ROWS_DEV, cols), bf16),
            pltpu.VMEM((chips, CORES, ROWS_DEV, cols), bf16),
            pltpu.VMEM((UNITS, chips, ROWS_DEV, span), f32),
            pltpu.VMEM((UNITS, chips, ROWS_DEV, span), f32),
            pltpu.VMEM((UNITS, chips, ROWS_DEV, span), f32),
            pltpu.VMEM((UNITS, chips, ROWS_DEV, span), bf16),
            pltpu.VMEM((UNITS, chips, ROWS_DEV, span), bf16),
            pltpu.VMEM((ROWS_DEV, span), bf16),
            pltpu.VMEM((ROWS_DEV, span), bf16),
            pltpu.VMEM((24, LANES), f32),
            pltpu.VMEM((basis, LANES, 2 * LANES), bf16),
            [pltpu.VMEM((2, tall + 32, cols), bf16)] * (basis // 2),
            pltpu.VMEM((ROWS_DEV, deep), f32),
            pltpu.VMEM((8, deep), f32),
            [pltpu.VMEM((2 * ROWS_DEV, deep), bf16)] * (visits if few else 1),
            pltpu.VMEM((ROWS_DEV, deep), bf16),
            dma((7,)),
            dma((2,)),
            dma((2,)),
            dma((chips, CORES)),
            dma((chips, CORES)),
            dma((UNITS, chips)),
            dma((UNITS, chips)),
            dma((UNITS, chips)),
            dma((UNITS, chips)),
            dma((1,)),
            dma((1,)),
        ],
        compiler_params=pltpu.CompilerParams(
            collective_id=0, has_side_effects=True, vmem_limit_bytes=62 * 1024 * 1024
        ),
    )(image, variance, mask_bits, boxes, row_filters, col_filters, coeffs)
    return (sums[0] / jnp.maximum(sums[1], 1.0), sums[1])


def solution(mesh):
    in_specs = (
        P("visit", None, "sky"),
        P("visit", None, "sky"),
        P("visit", None, "sky"),
        P("visit", None),
        P(),
        P(),
        P("visit", None, None),
    )
    out_specs = (P("visit", "sky"), P("visit", "sky"))
    return jax.shard_map(
        per_device, mesh=mesh, in_specs=in_specs, out_specs=out_specs, check_vma=False
    )
```

```python
import functools

import jax
import jax.numpy as jnp
from jax import lax
from jax.experimental import pallas as pl
from jax.experimental.pallas import tpu as pltpu
from jax.sharding import PartitionSpec as P

RAD = 20
ROWS_DEV = 48
REJECT = 7
LANES = 128
CORES = 2
LEAD = 8
TOP = 24
WIN = 2 * ROWS_DEV
UNITS = 2
PACK = 5
TERMS = 6
MESH = pl.DeviceIdType.MESH


def weight_of(plane):
    plane = plane.astype(jnp.float32)
    near = pl.reciprocal(plane, approx=True)
    return jnp.where(plane > 0, near * (2.0 - plane * near), 0.0)


def kernel(
    visits,
    skies,
    image_hbm,
    var_hbm,
    bits_hbm,
    boxes_hbm,
    rowf_hbm,
    colf_hbm,
    coef_hbm,
    sums_ref,
    image_ref,
    var_ref,
    bits_ref,
    boxes_ref,
    rowf_ref,
    colf_ref,
    coef_ref,
    edge_send,
    edge_got,
    wide,
    masked,
    got_var,
    own_pix,
    sib_send,
    sib_pix,
    pair_pix,
    got_pix,
    cross_pix,
    got_cross,
    filt,
    col_mats,
    passed,
    toeplitz,
    factors,
    row_mats,
    row_last,
    load_sem,
    halo_send,
    halo_recv,
    var_send,
    var_recv,
    sib_send_sem,
    sib_recv_sem,
    pix_send,
    pix_recv,
    cross_send,
    cross_recv,
):
    height, cols = var_ref.shape[1], var_ref.shape[2]
    width = cols * skies
    basis, taps = rowf_ref.shape
    blocks = cols // LANES
    inner, outer = units = list(range(1, blocks - 1)), [0, blocks - 1]
    per_unit = blocks // UNITS
    chips = visits // CORES
    few = chips == 4
    deep = basis * WIN
    f32, bf16 = jnp.float32, jnp.bfloat16
    v = lax.axis_index("visit")
    z = lax.axis_index("sky")
    chip = v // CORES
    core = lax.rem(v, CORES)
    sibling = chip * CORES + 1 - core
    has_l = z > 0
    has_r = z < skies - 1

    def chip_at(slot):
        if not few:
            return lax.rem(chip + slot + 1, chips)
        return [chips - 1 - chip, lax.rem(chip + 2, chips), chip + 1 - 2 * lax.rem(chip, 2), chip][slot]

    def each(first, last, body):
        if few:
            for slot in range(first, last):
                body(slot)
        else:

            def one(slot, carry):
                body(slot)
                return carry

            lax.fori_loop(first, last, one, 0)

    pairs = (
        (rowf_hbm, rowf_ref),
        (colf_hbm, colf_ref),
        (coef_hbm, coef_ref),
        (image_hbm.at[0], image_ref.at[pl.ds(16, height)]),
        (boxes_hbm, boxes_ref),
        (var_hbm, var_ref),
        (bits_hbm, bits_ref),
    )
    loads = [
        pltpu.make_async_copy(src, dst, load_sem.at[n]) for n, (src, dst) in enumerate(pairs)
    ]
    for load in loads:
        load.start()

    barrier = pltpu.get_barrier_semaphore()
    for step in range(1, visits):
        pl.semaphore_signal(
            barrier, inc=1, device_id=(lax.rem(v + step, visits), z), device_id_type=MESH
        )

    @pl.when(has_l)
    def _():
        pl.semaphore_signal(barrier, inc=1, device_id=(v, z - 1), device_id_type=MESH)

    @pl.when(has_r)
    def _():
        pl.semaphore_signal(barrier, inc=1, device_id=(v, z + 1), device_id_type=MESH)

    below = image_ref.shape[0] - 16 - height
    image_ref[0:16, :] = jnp.zeros((16, cols), bf16)
    image_ref[16 + height :, :] = jnp.zeros((below, cols), bf16)
    col_first = z * cols
    for pair in passed:
        for h in range(2):
            for k in range(blocks):
                pair[h, k, 0:16, :] = jnp.zeros((16, LANES), bf16)
                pair[h, k, pair.shape[2] - 16 :, :] = jnp.zeros((16, LANES), bf16)

    for load in loads[:3]:
        load.wait()
    filt[...] = jnp.zeros_like(filt)
    filt[0:basis, 0:taps] = colf_ref[...].astype(f32)
    lane = lax.broadcasted_iota(jnp.int32, (1, LANES), 1)
    ahead = lax.broadcasted_iota(jnp.int32, (LANES, LANES), 1) >= lax.broadcasted_iota(
        jnp.int32, (LANES, LANES), 0
    )

    def build(b):
        col = jnp.broadcast_to(filt[pl.ds(b, 1), :], (LANES, LANES))
        col = pltpu.roll(col, 0, 1, stride=1, stride_axis=0)
        col_mats[0, b] = jnp.where(ahead, col, 0.0).astype(bf16)
        col_mats[1, b] = jnp.where(ahead, 0.0, col).astype(bf16)

    group_of = lax.broadcasted_iota(jnp.int32, (1, deep), 1) // WIN
    tap_of = lax.broadcasted_iota(jnp.int32, (1, deep), 1) - group_of * WIN - (TOP - RAD)
    tap_mat = (lax.broadcasted_iota(jnp.int32, (taps, deep), 0) == tap_of).astype(f32).astype(bf16)
    own_group = (lax.broadcasted_iota(jnp.int32, (basis, deep), 0) == group_of).astype(f32)
    every = jnp.dot(rowf_ref[...], tap_mat, preferred_element_type=f32)
    line = jnp.sum(every * own_group, axis=0, keepdims=True)
    toeplitz[...] = pltpu.roll(
        jnp.broadcast_to(line, (ROWS_DEV, deep)), 0, 1, stride=1, stride_axis=0
    )
    c = jnp.dot(
        coef_ref[:, 0, :], own_group, precision=lax.Precision.HIGHEST, preferred_element_type=f32
    )
    c = [c[t : t + 1] for t in range(TERMS)]
    xc = (2 * col_first + cols).astype(f32) / width - 1.0
    factors[0:1] = c[0] + xc * (c[1] + xc * c[3])
    factors[1:2] = c[2] + xc * c[4]
    factors[2:3] = c[5]
    factors[3:4] = c[1] + (2.0 * xc) * c[3]
    factors[4:5] = c[4]
    last = (toeplitz[...] * c[3]).astype(bf16)
    for n in range(deep // LANES):
        row_last[n] = last[:, n * LANES : (n + 1) * LANES]
    y_iota = lax.broadcasted_iota(jnp.int32, (ROWS_DEV, LANES), 0)
    tiles = deep // LANES

    def build_rows(band, at, first, last, tie):
        y = (2.0 * (band * ROWS_DEV + y_iota).astype(f32) + 1.0) / height - 1.0 + tie
        for n in range(first, last):
            lanes = slice(n * LANES, (n + 1) * LANES)
            base = toeplitz[:, lanes]
            f = [factors[t : t + 1, lanes] for t in range(5)]
            row_mats[at][n, 0:ROWS_DEV, :] = (base * (f[0] + y * (f[1] + y * f[2]))).astype(bf16)
            row_mats[at][n, ROWS_DEV : 2 * ROWS_DEV, :] = (base * (f[3] + y * f[4])).astype(bf16)

    strip = wide.shape[1] // PACK
    loads[3].wait()
    to_l = to_r = jnp.zeros((strip, LANES), f32)
    for g in range(PACK):
        rows = slice(g * strip, (g + 1) * strip)
        ends = [
            image_ref[g * strip : (g + 1) * strip + 16, k * LANES : (k + 1) * LANES].astype(f32)
            for k in (blocks - 1, 0)
        ]
        edge = jnp.concatenate([end[LEAD : LEAD + strip] for end in ends], axis=1)
        edge = pltpu.roll(edge, RAD, 1)[:, LANES:]
        wide[blocks, rows, :] = edge.astype(bf16)
        at = g * RAD
        edge = pltpu.roll(edge, at, 1) if g else edge
        to_r = jnp.where((lane >= at) & (lane < at + RAD), edge, to_r)
        to_l = jnp.where((lane >= at + RAD) & (lane < at + 2 * RAD), edge, to_l)
    edge_send[0] = to_l.astype(bf16)
    edge_send[1] = to_r.astype(bf16)

    def remote(src, dst, send, recv, target):
        return pltpu.make_async_remote_copy(
            src_ref=src,
            dst_ref=dst,
            send_sem=send,
            recv_sem=recv,
            device_id=target,
            device_id_type=MESH,
        )

    def edge_copy(side, target):
        return remote(
            edge_send.at[side],
            edge_got.at[side],
            halo_send.at[side],
            halo_recv.at[side],
            (v, target),
        )

    def peer(slot):
        return (chip_at(slot) * CORES + core, z)

    def var_copy(slot, other):
        side = 1 - core if other else core
        return remote(
            masked.at[side, chip_at(slot)],
            got_var.at[slot, other],
            var_send.at[slot, other],
            var_recv.at[slot, other],
            (chip_at(slot) * CORES + side, z),
        )

    def for_vars(act):
        def both(slot):
            act(slot, 0)
            act(slot, 1)

        each(0, chips - 1, both)
        act(chips - 1, 1)

    def sib_copy(unit, slot):
        return remote(
            sib_send.at[unit, slot],
            sib_pix.at[unit, slot],
            sib_send_sem.at[unit, slot],
            sib_recv_sem.at[unit, slot],
            (sibling, z),
        )

    def pix_copy(unit, slot):
        return remote(
            pair_pix.at[unit, slot],
            got_pix.at[unit, slot],
            pix_send.at[unit, slot],
            pix_recv.at[unit, slot],
            peer(slot),
        )

    def cross_copy():
        target = (chip_at(2) * CORES + 1 - core, z)
        return remote(cross_pix, got_cross, cross_send.at[0], cross_recv.at[0], target)

    pl.semaphore_wait(barrier, visits - 1 + has_l.astype(jnp.int32) + has_r.astype(jnp.int32))

    @pl.when(has_l)
    def _():
        edge_copy(0, z - 1).start()

    @pl.when(has_r)
    def _():
        edge_copy(1, z + 1).start()

    for g in range(PACK):
        part = image_ref[g * strip : (g + 1) * strip + 16, :].astype(f32)[LEAD : LEAD + strip]
        part = pltpu.roll(part, RAD, 1)
        for k in range(1, blocks):
            wide[k, g * strip : (g + 1) * strip, :] = part[:, k * LANES : (k + 1) * LANES].astype(bf16)

    for load in loads[4:]:
        load.wait()
    box = [boxes_ref[0, i] for i in range(4)]
    col_index = col_first + lax.broadcasted_iota(jnp.int32, (1, cols), 1)
    col_out = jnp.where((col_index >= box[2]) & (col_index < box[3]), 0, 1)
    row_iota = lax.broadcasted_iota(jnp.int32, (ROWS_DEV, LANES), 0)

    def mask_band(band, carry):
        first = pl.multiple_of(band * ROWS_DEV, ROWS_DEV)
        rows = pl.ds(first, ROWS_DEV)
        row_index = first + row_iota
        row_out = jnp.where((row_index >= box[0]) & (row_index < box[1]), 0, 1)
        row_out = jnp.concatenate([row_out] * blocks, axis=1)
        out = (bits_ref[0, rows, :] & REJECT) | row_out | col_out
        masked[lax.rem(band, CORES), band // CORES] = jnp.where(
            out == 0, var_ref[0, rows, :].astype(f32), 0.0
        ).astype(bf16)
        return carry

    lax.fori_loop(0, visits, mask_band, 0, unroll=few)
    for_vars(lambda slot, other: var_copy(slot, other).start())

    def col_step(p, first, rows, which):
        parts = [
            jnp.concatenate([wide[k + n, pl.ds(first, rows), :] for n in range(2)], axis=1)
            for k in which
        ]
        mats = jnp.concatenate(
            [col_mats[n, pl.ds(2 * p, 2)].reshape(2 * LANES, LANES) for n in range(2)], axis=1
        )
        out = lax.dot_general(
            jnp.concatenate(parts, axis=0),
            mats,
            (((1,), (1,)), ((), ())),
            preferred_element_type=f32,
        )
        into = pl.ds(pl.multiple_of(first + 16, 16), rows)
        for n, k in enumerate(which):
            for h in range(2):
                passed[p][h, k, into, :] = out[
                    n * rows : (n + 1) * rows, h * LANES : (h + 1) * LANES
                ].astype(bf16)
        return out[0:1, 0:LANES] * 0.0

    def weighted(unit, slot, side, at):
        which = units[unit]
        at_chip = chip_at(slot)
        band = at_chip * CORES + side
        if not few:
            build_rows(band, at, 0, tiles, 0.0)
        rows = pl.ds(pl.multiple_of(band * ROWS_DEV, 16), WIN)
        mats = jnp.concatenate(
            [jnp.concatenate([row_mats[at][n], row_last[n]], axis=0) for n in range(tiles)], axis=1
        )
        lines = jnp.concatenate(
            [
                jnp.concatenate(
                    [
                        pair[:, k, rows, :].reshape(2 * WIN, LANES)
                        for pair in passed
                    ],
                    axis=0,
                )
                for k in which
            ],
            axis=1,
        )
        out = jnp.dot(mats, lines, preferred_element_type=f32)
        x = jnp.concatenate(
            [(2 * (k * LANES + lane) + 1 - cols).astype(f32) / width for k in which], axis=1
        )
        pixels = out[0:ROWS_DEV] + x * (
            out[ROWS_DEV : 2 * ROWS_DEV] + x * out[2 * ROWS_DEV : 3 * ROWS_DEV]
        )
        plane = masked[side, at_chip]
        plane = jnp.concatenate([plane[:, k * LANES : (k + 1) * LANES] for k in which], axis=1)
        return pixels * weight_of(plane), out[0:1, 0:LANES] * 0.0

    def for_sibling(unit, slot, at=0):
        sib_send[unit, slot], tie = weighted(unit, slot, 1 - core, at)
        return tie

    def for_own(unit, slot, at=0):
        own_pix[unit, slot], tie = weighted(unit, slot, core, at)
        return tie

    def send_pair(unit, slot):
        sib_copy(unit, slot).wait_recv()
        pair_pix[unit, slot] = (own_pix[unit, slot] + sib_pix[unit, slot]).astype(bf16)
        pix_copy(unit, slot).start()

    def edges():
        @pl.when(has_l)
        def _():
            edge_copy(1, z - 1).wait_recv()

        @pl.when(has_r)
        def _():
            edge_copy(0, z + 1).wait_recv()

        @pl.when(jnp.logical_not(has_l))
        def _():
            edge_got[1] = jnp.zeros((strip, LANES), bf16)

        @pl.when(jnp.logical_not(has_r))
        def _():
            edge_got[0] = jnp.zeros((strip, LANES), bf16)

    def merge_edges():
        for g in range(PACK):
            rows = slice(g * strip, (g + 1) * strip)
            mine = wide[blocks, rows, :].astype(f32)
            from_r, from_l = (edge_got[side].astype(f32) for side in range(2))
            if g:
                from_r = pltpu.roll(from_r, LANES - g * RAD, 1)
                from_l = pltpu.roll(from_l, LANES - g * RAD, 1)
            wide[0, rows, :] = jnp.where(lane < RAD, from_l, mine).astype(bf16)
            wide[blocks, rows, :] = jnp.where(
                (lane >= RAD) & (lane < 2 * RAD), from_r, mine
            ).astype(bf16)

    def add_weights():
        sums_ref[1] = weight_of(masked[core, chip])

        def one(slot, other):
            var_copy(slot, other).wait_recv()
            sums_ref[1] += weight_of(got_var[slot, other])

        for_vars(one)

    def in_place(plane_of):
        lanes_of = {}
        for unit, which in enumerate(units):
            part = plane_of(unit)
            for n, k in enumerate(which):
                lanes_of[k] = part[:, n * LANES : (n + 1) * LANES]
        return jnp.concatenate([lanes_of[k] for k in range(blocks)], axis=1)

    def add_to(unit, value, first=False):
        for n, k in enumerate(units[unit]):
            lanes = slice(k * LANES, (k + 1) * LANES)
            part = value[:, n * LANES : (n + 1) * LANES]
            sums_ref[0, :, lanes] = part if first else sums_ref[0, :, lanes] + part

    def add_own(unit):
        sib_copy(unit, chips - 1).wait_recv()
        add_to(unit, own_pix[unit, chips - 1] + sib_pix[unit, chips - 1], True)

    def add_pixels(unit, slot):
        pix_copy(unit, slot).wait_recv()
        add_to(unit, got_pix[unit, slot].astype(f32))

    steps = basis // 2
    if few:
        half = chips // 2 * CORES * ROWS_DEV
        group = chip // 2
        total = height + 2 * LEAD
        early = half + 2 * LEAD + LEAD * 2
        far = pl.multiple_of((1 - group) * (total - early), 16)
        near = pl.multiple_of(group * early, 16)
        bands = [(0, 1), (1, 1), (2, 1), (0, 0), (1, 0), (2, 0), (3, 1), (3, 0)]

        def band_of(at):
            slot, other = bands[at]
            return chip_at(slot) * CORES + (1 - core if other else core)

        def columns(first, rows, which, base, count, build_too=False, some=range(steps)):
            pieces = [(base + n // tiles, n % tiles) for n in range(count * tiles)]
            each_step = -(-len(pieces) // steps)
            for p in some:
                if build_too:
                    build(2 * p)
                    build(2 * p + 1)
                tie = col_step(p, first, rows, which)
                mine = pieces[p * each_step : (p + 1) * each_step]
                for at in sorted({at for at, _ in mine}):
                    of = [n for a, n in mine if a == at]
                    build_rows(band_of(at), at, of[0], of[-1] + 1, tie)

        def rows_beside(at, tie):
            build_rows(band_of(at), at, 0, tiles, tie)

        columns(far, early, inner, 0, 2, True)
        columns(near, total - early, inner, 2, 3)
        rows_beside(5, for_sibling(0, 0, 0))
        for_sibling(0, 1, 1)
        for_sibling(0, 2, 2)
        for_own(0, 0, 3)
        tie = for_own(0, 1, 4)
        rows_beside(6, tie)
        rows_beside(7, tie)
        for_own(0, 2, 5)
        edges()
        for slot in range(3):
            sib_copy(0, slot).start()
        merge_edges()
        columns(far, early, outer, 0, 0)
        for slot in range(2):
            for_sibling(1, slot, slot)
        for slot in range(2):
            sib_copy(1, slot).start()
        for slot in range(3):
            send_pair(0, slot)
        for slot in range(2):
            for_own(1, slot, 3 + slot)
        columns(near, total - early, outer, 0, 0, some=range(steps // 2))
        for slot in range(2):
            send_pair(1, slot)
        columns(near, total - early, outer, 0, 0, some=range(steps // 2, steps))
        cross_pix[...] = weighted(1, 2, 1 - core, 2)[0].astype(bf16)
        pair_pix[1, 2] = weighted(1, 2, core, 5)[0].astype(bf16)
        cross_copy().start()
        pix_copy(1, 2).start()
        for unit in range(UNITS):
            for_sibling(unit, 3, 6)
            for_own(unit, 3, 7)
        for unit in range(UNITS):
            sib_copy(unit, 3).start()
    else:
        edges()
        merge_edges()
        for b in range(basis):
            build(b)

        def one(g, carry):
            for p in range(steps):
                for which in units:
                    col_step(p, pl.multiple_of(g * strip, 16), strip, which)
            return carry

        lax.fori_loop(0, PACK, one, 0)
        for unit in range(UNITS):

            def sibling_band(slot):
                for_sibling(unit, slot)
                sib_copy(unit, slot).start()

            each(0, chips, sibling_band)
            each(0, chips, lambda slot: for_own(unit, slot))
            each(0, chips - 1, lambda slot: send_pair(unit, slot))

    add_weights()
    add_own(0)
    each(0, chips - 1, lambda slot: add_pixels(0, slot))
    add_own(1)

    for_vars(lambda slot, other: var_copy(slot, other).wait_send())

    def drain(slot):
        for unit in range(UNITS):
            pix_copy(unit, slot).wait_send()

    each(0, chips - 1, drain)
    for unit in range(UNITS):
        each(
            0,
            chips,
            lambda slot: None if few and (unit, slot) == (1, 2) else sib_copy(unit, slot).wait_send(),
        )

    @pl.when(has_l)
    def _():
        edge_copy(0, z - 1).wait_send()

    @pl.when(has_r)
    def _():
        edge_copy(1, z + 1).wait_send()

    if few:
        cross_copy().wait_send()
        add_pixels(1, 2)
        cross_copy().wait_recv()
        add_to(1, got_cross[...].astype(f32))
        add_pixels(1, 1)
        add_pixels(1, 0)
    else:
        each(0, chips - 1, lambda slot: add_pixels(1, slot))


def per_device(image, variance, mask_bits, boxes, row_filters, col_filters, coeffs):
    height, cols = image.shape[1], image.shape[2]
    visits, skies = lax.axis_size("visit"), lax.axis_size("sky")
    basis = row_filters.shape[0]
    chips = visits // CORES
    few = chips == 4
    deep = basis * WIN
    span = cols // UNITS
    unit = 16 * PACK
    tall = (height + 2 * LEAD + unit - 1) // unit * unit
    coeffs = jnp.transpose(coeffs, (2, 0, 1))
    hbm = pl.BlockSpec(memory_space=pltpu.HBM)
    f32, bf16 = jnp.float32, jnp.bfloat16
    dma = pltpu.SemaphoreType.DMA
    sums = pl.pallas_call(
        functools.partial(kernel, visits, skies),
        out_shape=jax.ShapeDtypeStruct((2, ROWS_DEV, cols), f32),
        in_specs=[hbm] * 7,
        out_specs=pl.BlockSpec(memory_space=pltpu.VMEM),
        scratch_shapes=[
            pltpu.VMEM((tall + 16, cols), bf16),
            pltpu.VMEM(variance.shape, bf16),
            pltpu.VMEM(mask_bits.shape, jnp.int32),
            pltpu.SMEM(boxes.shape, jnp.int32),
            pltpu.VMEM(row_filters.shape, bf16),
            pltpu.VMEM(col_filters.shape, bf16),
            pltpu.VMEM(coeffs.shape, f32),
            pltpu.VMEM((2, tall // PACK, LANES), bf16),
            pltpu.VMEM((2, tall // PACK, LANES), bf16),
            pltpu.VMEM((cols // LANES + 1, tall, LANES), bf16),
            pltpu.VMEM((CORES, chips, ROWS_DEV, cols), bf16),
            pltpu.VMEM((chips, CORES, ROWS_DEV, cols), bf16),
            pltpu.VMEM((UNITS, chips, ROWS_DEV, span), f32),
            pltpu.VMEM((UNITS, chips, ROWS_DEV, span), f32),
            pltpu.VMEM((UNITS, chips, ROWS_DEV, span), f32),
            pltpu.VMEM((UNITS, chips, ROWS_DEV, span), bf16),
            pltpu.VMEM((UNITS, chips, ROWS_DEV, span), bf16),
            pltpu.VMEM((ROWS_DEV, span), bf16),
            pltpu.VMEM((ROWS_DEV, span), bf16),
            pltpu.VMEM((24, LANES), f32),
            pltpu.VMEM((2, basis, LANES, LANES), bf16),
            [pltpu.VMEM((2, cols // LANES, tall + 32, LANES), bf16)] * (basis // 2),
            pltpu.VMEM((ROWS_DEV, deep), f32),
            pltpu.VMEM((8, deep), f32),
            [pltpu.VMEM((deep // LANES, 2 * ROWS_DEV, LANES), bf16)] * (visits if few else 1),
            pltpu.VMEM((deep // LANES, ROWS_DEV, LANES), bf16),
            dma((7,)),
            dma((2,)),
            dma((2,)),
            dma((chips, CORES)),
            dma((chips, CORES)),
            dma((UNITS, chips)),
            dma((UNITS, chips)),
            dma((UNITS, chips)),
            dma((UNITS, chips)),
            dma((1,)),
            dma((1,)),
        ],
        compiler_params=pltpu.CompilerParams(
            collective_id=0, has_side_effects=True, vmem_limit_bytes=62 * 1024 * 1024
        ),
    )(image, variance, mask_bits, boxes, row_filters, col_filters, coeffs)
    return (sums[0] / jnp.maximum(sums[1], 1.0), sums[1])


def solution(mesh):
    in_specs = (
        P("visit", None, "sky"),
        P("visit", None, "sky"),
        P("visit", None, "sky"),
        P("visit", None),
        P(),
        P(),
        P("visit", None, None),
    )
    out_specs = (P("visit", "sky"), P("visit", "sky"))
    return jax.shard_map(
        per_device, mesh=mesh, in_specs=in_specs, out_specs=out_specs, check_vma=False
    )
```

```python
import functools

import jax
import jax.numpy as jnp
from jax import lax
from jax.experimental import pallas as pl
from jax.experimental.pallas import tpu as pltpu
from jax.sharding import PartitionSpec as P

RAD = 20
ROWS_DEV = 48
REJECT = 7
LANES = 128
CORES = 2
LEAD = 8
TOP = 24
WIN = 2 * ROWS_DEV
UNITS = 2
PACK = 5
TERMS = 6
MESH = pl.DeviceIdType.MESH


def weight_of(plane):
    plane = plane.astype(jnp.float32)
    near = pl.reciprocal(plane, approx=True)
    return jnp.where(plane > 0, near * (2.0 - plane * near), 0.0)


def kernel(
    visits,
    skies,
    image_hbm,
    var_hbm,
    bits_hbm,
    boxes_hbm,
    rowf_hbm,
    colf_hbm,
    coef_hbm,
    sums_ref,
    image_ref,
    var_ref,
    bits_ref,
    boxes_ref,
    rowf_ref,
    colf_ref,
    coef_ref,
    edge_send,
    edge_got,
    wide,
    masked,
    got_var,
    own_pix,
    sib_send,
    sib_pix,
    pair_pix,
    got_pix,
    cross_pix,
    got_cross,
    filt,
    col_mats,
    passed,
    toeplitz,
    factors,
    row_mats,
    row_last,
    load_sem,
    halo_send,
    halo_recv,
    var_send,
    var_recv,
    sib_send_sem,
    sib_recv_sem,
    pix_send,
    pix_recv,
    cross_send,
    cross_recv,
):
    height, cols = var_ref.shape[1], var_ref.shape[2]
    width = cols * skies
    basis, taps = rowf_ref.shape
    blocks = cols // LANES
    inner, outer = units = list(range(1, blocks - 1)), [0, blocks - 1]
    per_unit = blocks // UNITS
    chips = visits // CORES
    few = chips == 4
    deep = basis * WIN
    f32, bf16 = jnp.float32, jnp.bfloat16
    v = lax.axis_index("visit")
    z = lax.axis_index("sky")
    chip = v // CORES
    core = lax.rem(v, CORES)
    sibling = chip * CORES + 1 - core
    has_l = z > 0
    has_r = z < skies - 1

    def chip_at(slot):
        if not few:
            return lax.rem(chip + slot + 1, chips)
        return [chips - 1 - chip, lax.rem(chip + 2, chips), chip + 1 - 2 * lax.rem(chip, 2), chip][slot]

    def each(first, last, body):
        if few:
            for slot in range(first, last):
                body(slot)
        else:

            def one(slot, carry):
                body(slot)
                return carry

            lax.fori_loop(first, last, one, 0)

    pairs = (
        (rowf_hbm, rowf_ref),
        (colf_hbm, colf_ref),
        (coef_hbm, coef_ref),
        (image_hbm.at[0], image_ref.at[pl.ds(16, height)]),
        (boxes_hbm, boxes_ref),
        (var_hbm, var_ref),
        (bits_hbm, bits_ref),
    )
    loads = [
        pltpu.make_async_copy(src, dst, load_sem.at[n]) for n, (src, dst) in enumerate(pairs)
    ]
    for load in loads:
        load.start()

    barrier = pltpu.get_barrier_semaphore()
    for step in range(1, visits):
        pl.semaphore_signal(
            barrier, inc=1, device_id=(lax.rem(v + step, visits), z), device_id_type=MESH
        )

    @pl.when(has_l)
    def _():
        pl.semaphore_signal(barrier, inc=1, device_id=(v, z - 1), device_id_type=MESH)

    @pl.when(has_r)
    def _():
        pl.semaphore_signal(barrier, inc=1, device_id=(v, z + 1), device_id_type=MESH)

    below = image_ref.shape[0] - 16 - height
    image_ref[0:16, :] = jnp.zeros((16, cols), bf16)
    image_ref[16 + height :, :] = jnp.zeros((below, cols), bf16)
    col_first = z * cols
    for pair in passed:
        for h in range(2):
            for k in range(blocks):
                pair[h, k, 0:16, :] = jnp.zeros((16, LANES), bf16)
                pair[h, k, pair.shape[2] - 16 :, :] = jnp.zeros((16, LANES), bf16)

    for load in loads[:3]:
        load.wait()
    filt[...] = jnp.zeros_like(filt)
    filt[0:basis, 0:taps] = colf_ref[...].astype(f32)
    lane = lax.broadcasted_iota(jnp.int32, (1, LANES), 1)
    ahead = lax.broadcasted_iota(jnp.int32, (LANES, LANES), 1) >= lax.broadcasted_iota(
        jnp.int32, (LANES, LANES), 0
    )

    def build(b):
        col = jnp.broadcast_to(filt[pl.ds(b, 1), :], (LANES, LANES))
        col = pltpu.roll(col, 0, 1, stride=1, stride_axis=0)
        col_mats[0, b] = jnp.where(ahead, col, 0.0).astype(bf16)
        col_mats[1, b] = jnp.where(ahead, 0.0, col).astype(bf16)

    group_of = lax.broadcasted_iota(jnp.int32, (1, deep), 1) // WIN
    tap_of = lax.broadcasted_iota(jnp.int32, (1, deep), 1) - group_of * WIN - (TOP - RAD)
    tap_mat = (lax.broadcasted_iota(jnp.int32, (taps, deep), 0) == tap_of).astype(f32).astype(bf16)
    own_group = (lax.broadcasted_iota(jnp.int32, (basis, deep), 0) == group_of).astype(f32)
    every = jnp.dot(rowf_ref[...], tap_mat, preferred_element_type=f32)
    line = jnp.sum(every * own_group, axis=0, keepdims=True)
    toeplitz[...] = pltpu.roll(
        jnp.broadcast_to(line, (ROWS_DEV, deep)), 0, 1, stride=1, stride_axis=0
    )
    c = jnp.dot(
        coef_ref[:, 0, :], own_group, precision=lax.Precision.HIGHEST, preferred_element_type=f32
    )
    c = [c[t : t + 1] for t in range(TERMS)]
    xc = (2 * col_first + cols).astype(f32) / width - 1.0
    factors[0:1] = c[0] + xc * (c[1] + xc * c[3])
    factors[1:2] = c[2] + xc * c[4]
    factors[2:3] = c[5]
    factors[3:4] = c[1] + (2.0 * xc) * c[3]
    factors[4:5] = c[4]
    last = (toeplitz[...] * c[3]).astype(bf16)
    for n in range(deep // LANES):
        row_last[n] = last[:, n * LANES : (n + 1) * LANES]
    y_iota = lax.broadcasted_iota(jnp.int32, (ROWS_DEV, LANES), 0)
    tiles = deep // LANES

    def build_rows(band, at, first, last, tie):
        y = (2.0 * (band * ROWS_DEV + y_iota).astype(f32) + 1.0) / height - 1.0 + tie
        for n in range(first, last):
            lanes = slice(n * LANES, (n + 1) * LANES)
            base = toeplitz[:, lanes]
            f = [factors[t : t + 1, lanes] for t in range(5)]
            row_mats[at][n, 0:ROWS_DEV, :] = (base * (f[0] + y * (f[1] + y * f[2]))).astype(bf16)
            row_mats[at][n, ROWS_DEV : 2 * ROWS_DEV, :] = (base * (f[3] + y * f[4])).astype(bf16)

    strip = wide.shape[1] // PACK
    loads[3].wait()
    to_l = to_r = jnp.zeros((strip, LANES), f32)
    for g in range(PACK):
        rows = slice(g * strip, (g + 1) * strip)
        ends = [
            image_ref[g * strip : (g + 1) * strip + 16, k * LANES : (k + 1) * LANES].astype(f32)
            for k in (blocks - 1, 0)
        ]
        edge = jnp.concatenate([end[LEAD : LEAD + strip] for end in ends], axis=1)
        edge = pltpu.roll(edge, RAD, 1)[:, LANES:]
        wide[blocks, rows, :] = edge.astype(bf16)
        at = g * RAD
        edge = pltpu.roll(edge, at, 1) if g else edge
        to_r = jnp.where((lane >= at) & (lane < at + RAD), edge, to_r)
        to_l = jnp.where((lane >= at + RAD) & (lane < at + 2 * RAD), edge, to_l)
    edge_send[0] = to_l.astype(bf16)
    edge_send[1] = to_r.astype(bf16)

    def remote(src, dst, send, recv, target):
        return pltpu.make_async_remote_copy(
            src_ref=src,
            dst_ref=dst,
            send_sem=send,
            recv_sem=recv,
            device_id=target,
            device_id_type=MESH,
        )

    def edge_copy(side, target):
        return remote(
            edge_send.at[side],
            edge_got.at[side],
            halo_send.at[side],
            halo_recv.at[side],
            (v, target),
        )

    def peer(slot):
        return (chip_at(slot) * CORES + core, z)

    def var_copy(slot, other):
        side = 1 - core if other else core
        return remote(
            masked.at[side, chip_at(slot)],
            got_var.at[slot, other],
            var_send.at[slot, other],
            var_recv.at[slot, other],
            (chip_at(slot) * CORES + side, z),
        )

    def for_vars(act):
        def both(slot):
            act(slot, 0)
            act(slot, 1)

        each(0, chips - 1, both)
        act(chips - 1, 1)

    def sib_copy(unit, slot):
        return remote(
            sib_send.at[unit, slot],
            sib_pix.at[unit, slot],
            sib_send_sem.at[unit, slot],
            sib_recv_sem.at[unit, slot],
            (sibling, z),
        )

    def pix_copy(unit, slot):
        return remote(
            pair_pix.at[unit, slot],
            got_pix.at[unit, slot],
            pix_send.at[unit, slot],
            pix_recv.at[unit, slot],
            peer(slot),
        )

    def cross_copy():
        target = (chip_at(2) * CORES + 1 - core, z)
        return remote(cross_pix, got_cross, cross_send.at[0], cross_recv.at[0], target)

    pl.semaphore_wait(barrier, visits - 1 + has_l.astype(jnp.int32) + has_r.astype(jnp.int32))

    @pl.when(has_l)
    def _():
        edge_copy(0, z - 1).start()

    @pl.when(has_r)
    def _():
        edge_copy(1, z + 1).start()

    for g in range(PACK):
        part = image_ref[g * strip : (g + 1) * strip + 16, :].astype(f32)[LEAD : LEAD + strip]
        part = pltpu.roll(part, RAD, 1)
        for k in range(1, blocks):
            wide[k, g * strip : (g + 1) * strip, :] = part[:, k * LANES : (k + 1) * LANES].astype(bf16)

    for load in loads[4:]:
        load.wait()
    box = [boxes_ref[0, i] for i in range(4)]
    col_index = col_first + lax.broadcasted_iota(jnp.int32, (1, cols), 1)
    col_out = jnp.where((col_index >= box[2]) & (col_index < box[3]), 0, 1)
    row_iota = lax.broadcasted_iota(jnp.int32, (ROWS_DEV, LANES), 0)

    def mask_band(band, carry):
        first = pl.multiple_of(band * ROWS_DEV, ROWS_DEV)
        rows = pl.ds(first, ROWS_DEV)
        row_index = first + row_iota
        row_out = jnp.where((row_index >= box[0]) & (row_index < box[1]), 0, 1)
        row_out = jnp.concatenate([row_out] * blocks, axis=1)
        out = (bits_ref[0, rows, :] & REJECT) | row_out | col_out
        masked[lax.rem(band, CORES), band // CORES] = jnp.where(
            out == 0, var_ref[0, rows, :].astype(f32), 0.0
        ).astype(bf16)
        return carry

    lax.fori_loop(0, visits, mask_band, 0, unroll=few)
    for_vars(lambda slot, other: var_copy(slot, other).start())

    def col_step(p, first, rows, which):
        parts = [
            jnp.concatenate([wide[k + n, pl.ds(first, rows), :] for n in range(2)], axis=1)
            for k in which
        ]
        mats = jnp.concatenate(
            [col_mats[n, pl.ds(2 * p, 2)].reshape(2 * LANES, LANES) for n in range(2)], axis=1
        )
        out = lax.dot_general(
            jnp.concatenate(parts, axis=0),
            mats,
            (((1,), (1,)), ((), ())),
            preferred_element_type=f32,
        )
        into = pl.ds(pl.multiple_of(first + 16, 16), rows)
        for n, k in enumerate(which):
            for h in range(2):
                passed[p][h, k, into, :] = out[
                    n * rows : (n + 1) * rows, h * LANES : (h + 1) * LANES
                ].astype(bf16)
        return out[0:1, 0:LANES] * 0.0

    def weighted(unit, slot, side, at):
        which = units[unit]
        at_chip = chip_at(slot)
        band = at_chip * CORES + side
        if not few:
            build_rows(band, at, 0, tiles, 0.0)
        rows = pl.ds(pl.multiple_of(band * ROWS_DEV, 16), WIN)
        mats = jnp.concatenate(
            [jnp.concatenate([row_mats[at][n], row_last[n]], axis=0) for n in range(tiles)], axis=1
        )
        lines = jnp.concatenate(
            [
                jnp.concatenate(
                    [
                        pair[:, k, rows, :].reshape(2 * WIN, LANES)
                        for pair in passed
                    ],
                    axis=0,
                )
                for k in which
            ],
            axis=1,
        )
        out = jnp.dot(mats, lines, preferred_element_type=f32)
        x = jnp.concatenate(
            [(2 * (k * LANES + lane) + 1 - cols).astype(f32) / width for k in which], axis=1
        )
        pixels = out[0:ROWS_DEV] + x * (
            out[ROWS_DEV : 2 * ROWS_DEV] + x * out[2 * ROWS_DEV : 3 * ROWS_DEV]
        )
        plane = masked[side, at_chip]
        plane = jnp.concatenate([plane[:, k * LANES : (k + 1) * LANES] for k in which], axis=1)
        return pixels * weight_of(plane), out[0:1, 0:LANES] * 0.0

    def for_sibling(unit, slot, at=0):
        sib_send[unit, slot], tie = weighted(unit, slot, 1 - core, at)
        return tie

    def for_own(unit, slot, at=0):
        own_pix[unit, slot], tie = weighted(unit, slot, core, at)
        return tie

    def send_pair(unit, slot):
        sib_copy(unit, slot).wait_recv()
        pair_pix[unit, slot] = (own_pix[unit, slot] + sib_pix[unit, slot]).astype(bf16)
        pix_copy(unit, slot).start()

    def edges():
        @pl.when(has_l)
        def _():
            edge_copy(1, z - 1).wait_recv()

        @pl.when(has_r)
        def _():
            edge_copy(0, z + 1).wait_recv()

        @pl.when(jnp.logical_not(has_l))
        def _():
            edge_got[1] = jnp.zeros((strip, LANES), bf16)

        @pl.when(jnp.logical_not(has_r))
        def _():
            edge_got[0] = jnp.zeros((strip, LANES), bf16)

    def merge_edges():
        for g in range(PACK):
            rows = slice(g * strip, (g + 1) * strip)
            mine = wide[blocks, rows, :].astype(f32)
            from_r, from_l = (edge_got[side].astype(f32) for side in range(2))
            if g:
                from_r = pltpu.roll(from_r, LANES - g * RAD, 1)
                from_l = pltpu.roll(from_l, LANES - g * RAD, 1)
            wide[0, rows, :] = jnp.where(lane < RAD, from_l, mine).astype(bf16)
            wide[blocks, rows, :] = jnp.where(
                (lane >= RAD) & (lane < 2 * RAD), from_r, mine
            ).astype(bf16)

    def add_weights():
        sums_ref[1] = weight_of(masked[core, chip])

        def one(slot, other):
            var_copy(slot, other).wait_recv()
            sums_ref[1] += weight_of(got_var[slot, other])

        for_vars(one)

    def in_place(plane_of):
        lanes_of = {}
        for unit, which in enumerate(units):
            part = plane_of(unit)
            for n, k in enumerate(which):
                lanes_of[k] = part[:, n * LANES : (n + 1) * LANES]
        return jnp.concatenate([lanes_of[k] for k in range(blocks)], axis=1)

    def add_to(unit, value, first=False):
        for n, k in enumerate(units[unit]):
            lanes = slice(k * LANES, (k + 1) * LANES)
            part = value[:, n * LANES : (n + 1) * LANES]
            sums_ref[0, :, lanes] = part if first else sums_ref[0, :, lanes] + part

    def add_own(unit):
        sib_copy(unit, chips - 1).wait_recv()
        add_to(unit, own_pix[unit, chips - 1] + sib_pix[unit, chips - 1], True)

    def add_pixels(unit, slot):
        pix_copy(unit, slot).wait_recv()
        add_to(unit, got_pix[unit, slot].astype(f32))

    steps = basis // 2
    if few:
        half = chips // 2 * CORES * ROWS_DEV
        group = chip // 2
        total = height + 2 * LEAD
        early = half + 2 * LEAD + LEAD * 2
        far = pl.multiple_of((1 - group) * (total - early), 16)
        near = pl.multiple_of(group * early, 16)
        bands = [(0, 1), (1, 1), (2, 1), (0, 0), (1, 0), (2, 0), (3, 1), (3, 0)]

        def band_of(at):
            slot, other = bands[at]
            return chip_at(slot) * CORES + (1 - core if other else core)

        def columns(first, rows, which, base, count, build_too=False):
            pieces = [(base + n // tiles, n % tiles) for n in range(count * tiles)]
            each_step = -(-len(pieces) // steps)
            for p in range(steps):
                if build_too:
                    build(2 * p)
                    build(2 * p + 1)
                tie = col_step(p, first, rows, which)
                mine = pieces[p * each_step : (p + 1) * each_step]
                for at in sorted({at for at, _ in mine}):
                    of = [n for a, n in mine if a == at]
                    build_rows(band_of(at), at, of[0], of[-1] + 1, tie)

        def rows_beside(at, tie):
            build_rows(band_of(at), at, 0, tiles, tie)

        columns(far, early, inner, 0, 2, True)
        columns(near, total - early, inner, 2, 3)
        rows_beside(5, for_sibling(0, 0, 0))
        for_sibling(0, 1, 1)
        for_sibling(0, 2, 2)
        for_own(0, 0, 3)
        tie = for_own(0, 1, 4)
        rows_beside(6, tie)
        rows_beside(7, tie)
        for_own(0, 2, 5)
        edges()
        for slot in range(3):
            sib_copy(0, slot).start()
        merge_edges()
        columns(far, early, outer, 0, 0)
        for slot in range(2):
            for_sibling(1, slot, slot)
        for slot in range(2):
            sib_copy(1, slot).start()
        for slot in range(3):
            send_pair(0, slot)
        for slot in range(2):
            for_own(1, slot, 3 + slot)
        columns(near, total - early, outer, 0, 0)
        for slot in range(2):
            send_pair(1, slot)
        cross_pix[...] = weighted(1, 2, 1 - core, 2)[0].astype(bf16)
        pair_pix[1, 2] = weighted(1, 2, core, 5)[0].astype(bf16)
        cross_copy().start()
        pix_copy(1, 2).start()
        for unit in range(UNITS):
            for_sibling(unit, 3, 6)
            for_own(unit, 3, 7)
        for unit in range(UNITS):
            sib_copy(unit, 3).start()
    else:
        edges()
        merge_edges()
        for b in range(basis):
            build(b)

        def one(g, carry):
            for p in range(steps):
                for which in units:
                    col_step(p, pl.multiple_of(g * strip, 16), strip, which)
            return carry

        lax.fori_loop(0, PACK, one, 0)
        for unit in range(UNITS):

            def sibling_band(slot):
                for_sibling(unit, slot)
                sib_copy(unit, slot).start()

            each(0, chips, sibling_band)
            each(0, chips, lambda slot: for_own(unit, slot))
            each(0, chips - 1, lambda slot: send_pair(unit, slot))

    add_weights()
    add_own(0)
    each(0, chips - 1, lambda slot: add_pixels(0, slot))
    add_own(1)

    for_vars(lambda slot, other: var_copy(slot, other).wait_send())

    def drain(slot):
        for unit in range(UNITS):
            pix_copy(unit, slot).wait_send()

    each(0, chips - 1, drain)
    for unit in range(UNITS):
        each(
            0,
            chips,
            lambda slot: None if few and (unit, slot) == (1, 2) else sib_copy(unit, slot).wait_send(),
        )

    @pl.when(has_l)
    def _():
        edge_copy(0, z - 1).wait_send()

    @pl.when(has_r)
    def _():
        edge_copy(1, z + 1).wait_send()

    if few:
        cross_copy().wait_send()
        add_pixels(1, 2)
        cross_copy().wait_recv()
        add_to(1, got_cross[...].astype(f32))
        add_pixels(1, 1)
        add_pixels(1, 0)
    else:
        each(0, chips - 1, lambda slot: add_pixels(1, slot))


def per_device(image, variance, mask_bits, boxes, row_filters, col_filters, coeffs):
    height, cols = image.shape[1], image.shape[2]
    visits, skies = lax.axis_size("visit"), lax.axis_size("sky")
    basis = row_filters.shape[0]
    chips = visits // CORES
    few = chips == 4
    deep = basis * WIN
    span = cols // UNITS
    unit = 16 * PACK
    tall = (height + 2 * LEAD + unit - 1) // unit * unit
    coeffs = jnp.transpose(coeffs, (2, 0, 1))
    hbm = pl.BlockSpec(memory_space=pltpu.HBM)
    f32, bf16 = jnp.float32, jnp.bfloat16
    dma = pltpu.SemaphoreType.DMA
    sums = pl.pallas_call(
        functools.partial(kernel, visits, skies),
        out_shape=jax.ShapeDtypeStruct((2, ROWS_DEV, cols), f32),
        in_specs=[hbm] * 7,
        out_specs=pl.BlockSpec(memory_space=pltpu.VMEM),
        scratch_shapes=[
            pltpu.VMEM((tall + 16, cols), bf16),
            pltpu.VMEM(variance.shape, bf16),
            pltpu.VMEM(mask_bits.shape, jnp.int32),
            pltpu.SMEM(boxes.shape, jnp.int32),
            pltpu.VMEM(row_filters.shape, bf16),
            pltpu.VMEM(col_filters.shape, bf16),
            pltpu.VMEM(coeffs.shape, f32),
            pltpu.VMEM((2, tall // PACK, LANES), bf16),
            pltpu.VMEM((2, tall // PACK, LANES), bf16),
            pltpu.VMEM((cols // LANES + 1, tall, LANES), bf16),
            pltpu.VMEM((CORES, chips, ROWS_DEV, cols), bf16),
            pltpu.VMEM((chips, CORES, ROWS_DEV, cols), bf16),
            pltpu.VMEM((UNITS, chips, ROWS_DEV, span), f32),
            pltpu.VMEM((UNITS, chips, ROWS_DEV, span), f32),
            pltpu.VMEM((UNITS, chips, ROWS_DEV, span), f32),
            pltpu.VMEM((UNITS, chips, ROWS_DEV, span), bf16),
            pltpu.VMEM((UNITS, chips, ROWS_DEV, span), bf16),
            pltpu.VMEM((ROWS_DEV, span), bf16),
            pltpu.VMEM((ROWS_DEV, span), bf16),
            pltpu.VMEM((24, LANES), f32),
            pltpu.VMEM((2, basis, LANES, LANES), bf16),
            [pltpu.VMEM((2, cols // LANES, tall + 32, LANES), bf16)] * (basis // 2),
            pltpu.VMEM((ROWS_DEV, deep), f32),
            pltpu.VMEM((8, deep), f32),
            [pltpu.VMEM((deep // LANES, 2 * ROWS_DEV, LANES), bf16)] * (visits if few else 1),
            pltpu.VMEM((deep // LANES, ROWS_DEV, LANES), bf16),
            dma((7,)),
            dma((2,)),
            dma((2,)),
            dma((chips, CORES)),
            dma((chips, CORES)),
            dma((UNITS, chips)),
            dma((UNITS, chips)),
            dma((UNITS, chips)),
            dma((UNITS, chips)),
            dma((1,)),
            dma((1,)),
        ],
        compiler_params=pltpu.CompilerParams(
            collective_id=0, has_side_effects=True, vmem_limit_bytes=62 * 1024 * 1024
        ),
    )(image, variance, mask_bits, boxes, row_filters, col_filters, coeffs)
    return (sums[0] / jnp.maximum(sums[1], 1.0), sums[1])


def solution(mesh):
    in_specs = (
        P("visit", None, "sky"),
        P("visit", None, "sky"),
        P("visit", None, "sky"),
        P("visit", None),
        P(),
        P(),
        P("visit", None, None),
    )
    out_specs = (P("visit", "sky"), P("visit", "sky"))
    return jax.shard_map(
        per_device, mesh=mesh, in_specs=in_specs, out_specs=out_specs, check_vma=False
    )
```
